256 devices in a mesh: level: 32 (over z, y_hi, core), tensor: 8 (over x, y_lo).
Axes of the slice: x: 4, y: 4 (y_hi: 2, y_lo: 2; y = y_hi * 2 + y_lo), z: 8, core: 2. Of those that a mesh axis runs over, the one named last changes fastest.
Arguments:
- queue: bfloat16 [4096, 5120], P('level'), may hold values from -6 to 6
- tail_noise: bfloat16 [2, 128, 5120], P(None, 'tensor'), may hold values from -6 to 6
- timesteps: int32 [32], P('level'), may hold values from 15 to 991, as said below
- offsets: int32 [32], P('level'), may hold values from 0 to 128
- mod_table: float32 [3, 5120], replicated, may hold values from -3 to 3
- w_query: bfloat16 [5120, 3072], P('level', 'tensor')
- w_key: bfloat16 [5120, 3072], P('level', 'tensor')
- w_value: bfloat16 [5120, 3072], P('level', 'tensor'), may hold values from -0.078125 to 0.078125
- w_out: bfloat16 [3072, 5120], P('tensor', 'level'), may hold values from -0.109375 to 0.109375
Outputs:
- queue_out: bfloat16 [4096, 5120], P(('level', 'tensor'))
- velocities: bfloat16 [2, 4096, 5120], P(None, ('level', 'tensor'))
The draws below stay inside these ranges and needn't reach their ends.
Inputs may be any that keep to these rules, and one draw needn't show every extreme that they name: timesteps[j] lies in [j * 31 + 31 // 2, (j + 1) * 31).
All inputs are finite; a program needn't handle non-finite values.
Results may differ from the reference program's by a relative error of at most 0.023.
Values may be sent and summed in bfloat16 or wider, within the bound.
No kernel may reach another device: no remote copies, remote signals or barrier semaphores. Data moves between devices by JAX's collectives and lax.ppermute only.
A program may use at most 64 MiB of HBM per device.

```python
import math
import jax
import jax.numpy as jnp
from jax import lax

D = 5120
HEADS = 24
HD = 128
TOK_SEC = 128
TSTEPS = 1000
LEVELS = 32
INNER = 3072
N_TENSOR = 8


def shared_keys(key):
    return jax.random.normal(key, (D, INNER), jnp.float32) * D ** (-0.5)


def draw_w_key(key, part):
    return shared_keys(key).astype(jnp.bfloat16)


def draw_w_query(key, part):
    key = jax.random.fold_in(key, 11)
    own = jax.random.normal(key, (D, INNER), jnp.float32) * D ** (-0.5)
    return own.astype(jnp.bfloat16)


def draw_timesteps(key, part):
    key = jax.random.fold_in(key, 5)
    spacing = TSTEPS // LEVELS
    extra = jax.random.randint(key, (LEVELS,), spacing // 2, spacing)
    return (jnp.arange(LEVELS, dtype=jnp.int32) * spacing + extra).astype(jnp.int32)


def set_ends(values, rng, low, top_value):
    longest = values.shape.index(max(values.shape))
    spots = []
    for shift in (0, 1):
        where = [jax.random.randint(jax.random.fold_in(rng, axis), (), 0, length) for axis, length in enumerate(values.shape)]
        where[longest] = (where[longest] + shift) % values.shape[longest]
        spots.append(tuple(where))
    return values.at[spots[0]].set(low).at[spots[1]].set(top_value)


def shard_levels(rng, shape, pieces, low, largest):
    level, own = 1.0, jax.random.fold_in(rng, 6)
    for axis_at, shards_of in pieces:
        steps = jnp.exp(jax.random.uniform(jax.random.fold_in(own, axis_at), (shards_of,), jnp.float32, low / len(pieces), largest / len(pieces)))
        level = level * jnp.repeat(steps, shape[axis_at] // shards_of).reshape([-1 if axis == axis_at else 1 for axis in range(len(shape))])
    return level


def bell_draw(rng, shape, scale, limit, split=(), kind=jnp.bfloat16):
    gain = shard_levels(rng, shape, split, -0.22, 0.18) if split else 1.0
    entries = jax.random.normal(rng, shape, jnp.float32) * scale * gain
    return jnp.minimum(jnp.maximum(entries, -limit), limit).astype(kind)


def setup_inputs(seed: int = 0) -> dict:
    splits = jax.random.split(jax.random.key(seed), 10)
    return {
        "queue": bell_draw(splits[0], (LEVELS * TOK_SEC, D), 1.0, 6.0, ((0, 32),)),
        "tail_noise": bell_draw(splits[1], (2, TOK_SEC, D), 1.0, 6.0, ((1, 8),)),
        "timesteps": draw_timesteps(jax.random.fold_in(splits[9], 71), 0),
        "offsets": set_ends(jax.random.randint(splits[3], (LEVELS,), 0, TOK_SEC + 1), jax.random.fold_in(splits[3], 1), 0, TOK_SEC).astype(jnp.int32),
        "mod_table": bell_draw(splits[4], (3, D), 0.5, 3.0, (), jnp.float32),
        "w_query": draw_w_query(jax.random.fold_in(splits[9], 71), 0),
        "w_key": draw_w_key(jax.random.fold_in(splits[9], 71), 0),
        "w_value": bell_draw(splits[7], (D, INNER), D ** -0.5, 0.078125, ((0, 32), (1, 8))),
        "w_out": bell_draw(splits[8], (INNER, D), INNER ** -0.5, 0.109375, ((0, 8), (1, 32))),
    }


def sigma_of(t_index):
    unit = t_index.astype(jnp.float32) / TSTEPS
    return 5.0 * unit / (1.0 + 4.0 * unit)

def embed(t_index):
    half = D // 2
    freqs = jnp.exp(-math.log(10000.0) * jnp.arange(half, dtype=jnp.float32) / half)
    angles = t_index.astype(jnp.float32) * freqs
    return jnp.concatenate([jnp.sin(angles), jnp.cos(angles)])

def one_step(queue_now, timesteps, offsets, mod_table, w_query, w_key, w_value, w_out):
    levels = timesteps.shape[0]
    emb = jax.vmap(embed)(timesteps)
    x_float = queue_now.reshape(levels, TOK_SEC, D).astype(jnp.float32)
    mean = lax.optimization_barrier(jnp.mean(x_float, axis=-1, keepdims=True))
    var = lax.optimization_barrier(jnp.mean((x_float - mean) ** 2, axis=-1, keepdims=True))
    unit = (x_float - mean) / jnp.sqrt(var + 1e-06)
    normed = unit * (1.0 + mod_table[1] + 0.5 * emb[:, None, :]) + mod_table[0] + emb[:, None, :]
    normed = normed.astype(jnp.bfloat16).reshape(levels * TOK_SEC, D)
    query = jnp.dot(normed, w_query, preferred_element_type=jnp.float32).astype(jnp.bfloat16)
    keys = jnp.dot(normed, w_key, preferred_element_type=jnp.float32).astype(jnp.bfloat16)
    values = jnp.dot(normed, w_value, preferred_element_type=jnp.float32).astype(jnp.bfloat16)
    query = query.reshape(levels, TOK_SEC, HEADS, HD)
    keys = jnp.pad(keys.reshape(levels, TOK_SEC, HEADS, HD), ((1, 1), (0, 0), (0, 0), (0, 0)))
    values = jnp.pad(values.reshape(levels, TOK_SEC, HEADS, HD), ((1, 1), (0, 0), (0, 0), (0, 0)))
    key_win = jnp.concatenate([keys[:-2], keys[1:-1], keys[2:]], axis=1)
    val_win = jnp.concatenate([values[:-2], values[1:-1], values[2:]], axis=1)
    scores = jnp.einsum('lqhd,lkhd->lhqk', query.astype(jnp.float32), key_win.astype(jnp.float32)) / math.sqrt(HD)
    rows = jnp.arange(3 * TOK_SEC)[None, :]
    section = jnp.arange(levels)[:, None]
    live = (rows >= offsets[:, None]) & (rows < offsets[:, None] + 2 * TOK_SEC)
    live = live & ((rows >= TOK_SEC) | (section > 0)) & ((rows < 2 * TOK_SEC) | (section < levels - 1))
    live = live[:, None, None, :]
    scores = jnp.where(live, scores, -1e+30)
    top = lax.optimization_barrier(jnp.max(scores, axis=-1, keepdims=True))
    expo = jnp.where(live, jnp.exp(scores - top), 0.0)
    probs = (expo / lax.optimization_barrier(jnp.sum(expo, axis=-1, keepdims=True))).astype(jnp.bfloat16)
    attended = jnp.einsum('lhqk,lkhd->lqhd', probs.astype(jnp.float32), val_win.astype(jnp.float32))
    attended = attended.astype(jnp.bfloat16).reshape(levels * TOK_SEC, INNER)
    cols = INNER // N_TENSOR
    proj = jnp.zeros((levels * TOK_SEC, D), jnp.float32)
    for group in range(N_TENSOR):
        part = jnp.dot(attended[:, group * cols:(group + 1) * cols], w_out[group * cols:(group + 1) * cols], preferred_element_type=jnp.float32)
        part = lax.optimization_barrier(part.astype(jnp.bfloat16))
        proj = proj + part.astype(jnp.float32)
    proj = proj.reshape(levels, TOK_SEC, D)
    vel = (mod_table[2] + emb[:, None, :]) * proj
    gap = TSTEPS // levels
    delta = sigma_of(jnp.maximum(timesteps - gap, 0)) - sigma_of(timesteps)
    updated = (x_float + delta[:, None, None] * vel).astype(jnp.bfloat16)
    return (updated.reshape(levels * TOK_SEC, D), vel.astype(jnp.bfloat16).reshape(levels * TOK_SEC, D))

def reference(queue, tail_noise, timesteps, offsets, mod_table, w_query, w_key, w_value, w_out):
    current = queue
    vel_list = []
    for step in range(2):
        updated, vel = one_step(current, timesteps, offsets, mod_table, w_query, w_key, w_value, w_out)
        vel_list.append(vel)
        current = jnp.concatenate([updated[TOK_SEC:], tail_noise[step]], axis=0)
    return (current, jnp.stack(vel_list))
```

```python
import math

import jax
import jax.numpy as jnp
from jax import lax
from jax.sharding import PartitionSpec as P

D = 5120
HD = 128
TSTEPS = 1000
PLANES = 8
FLOAT = jnp.float32


def sigma_of(t_index):
    unit = t_index.astype(FLOAT) / TSTEPS
    return 5.0 * unit / (1.0 + 4.0 * unit)


def embed(t_index):
    half = D // 2
    freqs = jnp.exp(-math.log(10000.0) * jnp.arange(half, dtype=FLOAT) / half)
    angles = t_index.astype(FLOAT) * freqs
    return jnp.concatenate([jnp.sin(angles), jnp.cos(angles)])


def dot(a, b):
    return jnp.dot(a, b, preferred_element_type=FLOAT)


def dot_t(a, b):
    return lax.dot_general(a, b, (((1,), (1,)), ((), ())), preferred_element_type=FLOAT)


def to_z(block, hops):
    count = lax.axis_size("level")
    return lax.ppermute(block, "level", [(i, (i + 4 * hops) % count) for i in range(count)])


def swap(block, axis, bit):
    return lax.ppermute(block, axis, [(i, i ^ bit) for i in range(lax.axis_size(axis))])


def in_order(own, other, bit, axis=0):
    return jnp.where(
        bit == 0,
        jnp.concatenate([own, other], axis=axis),
        jnp.concatenate([other, own], axis=axis),
    )


def ring(block):
    rows = block.shape[0]
    out = {0: block}
    up = down = block
    for s in range(1, PLANES // 2):
        up, down = to_z(up, 1), to_z(down, -1)
        out[s], out[PLANES - s] = up, down
    far_up, far_down = to_z(up[: rows // 2], 1), to_z(down[rows // 2 :], -1)
    out[PLANES // 2] = jnp.concatenate([far_up, far_down])
    return out


def gather_early(first, second, y_hi, core):
    mine = jnp.where(core == 0, first, second)
    block = in_order(mine, swap(jnp.where(core == 0, second, first), "level", 1), core)
    block = in_order(block, swap(block, "level", 2), y_hi)
    blocks = ring(block)
    return [(blocks[s], swap(blocks[s], "level", 1)) for s in range(PLANES)]


def gather_late(shard, y_hi, core):
    blocks = ring(shard)
    out = []
    for s in range(PLANES):
        pair = in_order(blocks[s][None], swap(blocks[s], "level", 2)[None], y_hi)
        both = in_order(pair[:, None], swap(pair, "level", 1)[:, None], core, axis=1)
        out.append(both.reshape(4 * shard.shape[0], shard.shape[1]))
    return out


def normalize(x_float, emb, mod_table):
    mean = jnp.mean(x_float, axis=-1, keepdims=True)
    var = jnp.mean((x_float - mean) ** 2, axis=-1, keepdims=True)
    unit = (x_float - mean) / jnp.sqrt(var + 1e-06)
    return (unit * (1.0 + mod_table[1] + 0.5 * emb) + mod_table[0] + emb).astype(jnp.bfloat16)


def attend(query, keys, values, offset, tensor_id):
    rows_sec = query.shape[0]
    heads = query.shape[1] // HD
    level_id = lax.axis_index("level")
    level_count = lax.axis_size("level")
    up = [(i, i + 1) for i in range(level_count - 1)]
    down = [(i + 1, i) for i in range(level_count - 1)]
    stacked = jnp.stack((keys, values))
    window = jnp.concatenate(
        [lax.ppermute(stacked, "level", up), stacked, lax.ppermute(stacked, "level", down)], axis=1
    )
    query = query.reshape(rows_sec, heads, HD)
    key_win = window[0].reshape(3 * rows_sec, heads, HD)
    val_win = window[1].reshape(3 * rows_sec, heads, HD)
    scores = jnp.einsum("qhd,khd->hqk", query, key_win, preferred_element_type=FLOAT) / math.sqrt(
        HD
    )
    place = jnp.arange(3 * rows_sec)
    rows = place ^ (tensor_id * 16)
    live = (rows >= offset) & (rows < offset + 2 * rows_sec)
    live = (
        live
        & ((rows >= rows_sec) | (level_id > 0))
        & ((rows < 2 * rows_sec) | (level_id < level_count - 1))
    )
    live = live[None, None, :]
    scores = jnp.where(live, scores, -1e30)
    top = jnp.max(scores, axis=-1, keepdims=True)
    expo = jnp.where(live, jnp.exp(scores - top), 0.0)
    probs = (expo / jnp.sum(expo, axis=-1, keepdims=True)).astype(jnp.bfloat16)
    attended = jnp.einsum("hqk,khd->qhd", probs, val_win, preferred_element_type=FLOAT)
    return attended.astype(jnp.bfloat16).reshape(rows_sec, heads * HD)


def shards(queue, tail_noise, timesteps, offsets, mod_table, w_query, w_key, w_value, w_out):
    level_id = lax.axis_index("level")
    level_count = lax.axis_size("level")
    tensor_id = lax.axis_index("tensor")
    groups = lax.axis_size("tensor")
    z, y_hi, core = level_id // 4, (level_id // 2) % 2, level_id % 2
    share = queue.shape[0] // groups
    plane = D // PLANES

    qk_blocks = gather_early(w_query, w_key, y_hi, core)
    v_blocks = gather_late(w_value, y_hi, core)
    o_blocks = gather_late(w_out.T, y_hi, core)

    t_now = timesteps[0]
    emb = embed(t_now)
    gate = mod_table[2] + emb
    delta = sigma_of(jnp.maximum(t_now - TSTEPS // level_count, 0)) - sigma_of(t_now)
    is_last = level_id == level_count - 1

    def rolled(a):
        parts = [
            lax.dynamic_slice_in_dim(a, ((z - s) % PLANES) * plane, plane, 1)
            for s in range(PLANES)
        ]
        return jnp.concatenate(parts, axis=1)

    normed = normalize(queue.astype(FLOAT), emb, mod_table)
    normed = jnp.concatenate(
        [
            lax.dynamic_slice_in_dim(normed, (tensor_id ^ d) * share, share, 0)
            for d in range(groups)
        ]
    )
    normed = rolled(normed)
    current = lax.dynamic_slice_in_dim(queue, tensor_id * share, share, 0)
    vel_list = []
    for step in range(2):
        mine = other = value = 0.0
        for s in range(PLANES):
            x_part = normed[:, s * plane : (s + 1) * plane]
            mine = mine + dot(x_part, qk_blocks[s][0])
            other = other + dot(x_part, qk_blocks[s][1])
            value = value + dot(x_part, v_blocks[s])
        query = jnp.where(core == 0, mine, other).astype(jnp.bfloat16)
        keys = jnp.where(core == 0, other, mine).astype(jnp.bfloat16)
        attended = attend(query, keys, value.astype(jnp.bfloat16), offsets[0], tensor_id)
        part = jnp.concatenate(
            [dot_t(attended, o_blocks[s]).astype(jnp.bfloat16) for s in range(PLANES)], axis=1
        )
        proj = part[:share].astype(FLOAT)
        for d in range(1, groups):
            proj = proj + swap(part[d * share : (d + 1) * share], "tensor", d).astype(FLOAT)
        vel = gate * rolled(proj)
        updated = (current.astype(FLOAT) + delta * vel).astype(jnp.bfloat16)
        vel_list.append(vel.astype(jnp.bfloat16))
        moved = lax.ppermute(updated, "level", [(i + 1, i) for i in range(level_count - 1)])
        current = jnp.where(is_last, tail_noise[step], moved)
        if step == 0:
            own = rolled(normalize(current.astype(FLOAT), emb, mod_table))
            normed = jnp.concatenate(
                [own] + [swap(own, "tensor", d) for d in range(1, groups)], axis=0
            )
    return (current, jnp.stack(vel_list))


def solution(mesh):
    in_specs = (
        P("level", None),
        P(None, "tensor", None),
        P("level"),
        P("level"),
        P(),
        P("level", "tensor"),
        P("level", "tensor"),
        P("level", "tensor"),
        P("tensor", "level"),
    )
    out_specs = (P(("level", "tensor"), None), P(None, ("level", "tensor"), None))
    return jax.shard_map(shards, mesh=mesh, in_specs=in_specs, out_specs=out_specs, check_vma=False)
```

```python
import math

import jax
import jax.numpy as jnp
from jax import lax
from jax.sharding import PartitionSpec as P

D = 5120
HD = 128
TSTEPS = 1000
PLANES = 8
ORDER = (0, 1, 7, 2, 6, 3, 5, 4)
FLOAT = jnp.float32


def sigma_of(t_index):
    unit = t_index.astype(FLOAT) / TSTEPS
    return 5.0 * unit / (1.0 + 4.0 * unit)


def embed(t_index):
    half = D // 2
    freqs = jnp.exp(-math.log(10000.0) * jnp.arange(half, dtype=FLOAT) / half)
    angles = t_index.astype(FLOAT) * freqs
    return jnp.concatenate([jnp.sin(angles), jnp.cos(angles)])


def dot(a, b):
    return jnp.dot(a, b, preferred_element_type=FLOAT)


def dot_t(a, b):
    return lax.dot_general(a, b, (((1,), (1,)), ((), ())), preferred_element_type=FLOAT)


def to_z(block, hops):
    count = lax.axis_size("level")
    return lax.ppermute(block, "level", [(i, (i + 4 * hops) % count) for i in range(count)])


def swap(block, axis, bit):
    return lax.ppermute(block, axis, [(i, i ^ bit) for i in range(lax.axis_size(axis))])


def in_order(own, other, bit, axis=0):
    return jnp.where(
        bit == 0,
        jnp.concatenate([own, other], axis=axis),
        jnp.concatenate([other, own], axis=axis),
    )


def ring(block):
    rows = block.shape[0]
    out = {0: block}
    up = down = block
    for s in range(1, PLANES // 2):
        up, down = to_z(up, 1), to_z(down, -1)
        out[s], out[PLANES - s] = up, down
    far_up, far_down = to_z(up[: rows // 2], 1), to_z(down[rows // 2 :], -1)
    out[PLANES // 2] = jnp.concatenate([far_up, far_down])
    return out


def gather_weights(w_query, w_key, w_value, w_out_t, y_hi, core):
    query_value = jnp.concatenate([w_query, w_value], axis=1)
    key_out = jnp.concatenate([w_key, w_out_t], axis=1)
    mine = jnp.where(core == 0, query_value, key_out)
    pair = in_order(mine, swap(jnp.where(core == 0, key_out, query_value), "level", 1), core)
    wide = pair.shape[1] // 2
    early, late = pair[:, :wide], pair[:, wide:]
    late_blocks = ring(late)
    early_blocks = ring(in_order(early, swap(early, "level", 2), y_hi))
    rows = late.shape[0]
    crossed = {}
    for group in ((0,), (1, 7), (2, 6), (3, 5), (4,)):
        sent = jnp.concatenate([late_blocks[s] for s in group])
        got = swap(sent, "level", 2)
        for i, s in enumerate(group):
            crossed[s] = in_order(late_blocks[s], got[i * rows : (i + 1) * rows], y_hi)
    out = {}
    for s in ORDER:
        other = swap(crossed[s], "level", 1)
        value = jnp.where(core == 0, crossed[s], other)
        out_t = jnp.where(core == 0, other, crossed[s])
        out[s] = (early_blocks[s], swap(early_blocks[s], "level", 1), value, out_t)
    return out


def normalize(x_float, emb, mod_table):
    mean = jnp.mean(x_float, axis=-1, keepdims=True)
    var = jnp.mean((x_float - mean) ** 2, axis=-1, keepdims=True)
    unit = (x_float - mean) / jnp.sqrt(var + 1e-06)
    return (unit * (1.0 + mod_table[1] + 0.5 * emb) + mod_table[0] + emb).astype(jnp.bfloat16)


def attend(query, keys, values, offset, tensor_id):
    rows_sec = query.shape[0]
    heads = query.shape[1] // HD
    level_id = lax.axis_index("level")
    level_count = lax.axis_size("level")
    up = [(i, i + 1) for i in range(level_count - 1)]
    down = [(i + 1, i) for i in range(level_count - 1)]
    stacked = jnp.stack((keys, values))
    window = jnp.concatenate(
        [lax.ppermute(stacked, "level", up), stacked, lax.ppermute(stacked, "level", down)], axis=1
    )
    query = query.reshape(rows_sec, heads, HD)
    key_win = window[0].reshape(3 * rows_sec, heads, HD)
    val_win = window[1].reshape(3 * rows_sec, heads, HD)
    scores = jnp.einsum("qhd,khd->hqk", query, key_win, preferred_element_type=FLOAT) / math.sqrt(
        HD
    )
    place = jnp.arange(3 * rows_sec)
    rows = place ^ (tensor_id * 16)
    live = (rows >= offset) & (rows < offset + 2 * rows_sec)
    live = (
        live
        & ((rows >= rows_sec) | (level_id > 0))
        & ((rows < 2 * rows_sec) | (level_id < level_count - 1))
    )
    live = live[None, None, :]
    scores = jnp.where(live, scores, -1e30)
    top = jnp.max(scores, axis=-1, keepdims=True)
    expo = jnp.where(live, jnp.exp(scores - top), 0.0)
    probs = (expo / jnp.sum(expo, axis=-1, keepdims=True)).astype(jnp.bfloat16)
    attended = jnp.einsum("hqk,khd->qhd", probs, val_win, preferred_element_type=FLOAT)
    return attended.astype(jnp.bfloat16).reshape(rows_sec, heads * HD)


def shards(queue, tail_noise, timesteps, offsets, mod_table, w_query, w_key, w_value, w_out):
    level_id = lax.axis_index("level")
    level_count = lax.axis_size("level")
    tensor_id = lax.axis_index("tensor")
    groups = lax.axis_size("tensor")
    z, y_hi, core = level_id // 4, (level_id // 2) % 2, level_id % 2
    share = queue.shape[0] // groups
    plane = D // PLANES

    blocks = gather_weights(w_query, w_key, w_value, w_out.T, y_hi, core)
    shape = (D, w_query.shape[1])
    full = [jnp.zeros(shape, w_query.dtype) for _ in range(4)]
    for s in ORDER:
        full = [
            lax.dynamic_update_slice(whole, block, (s * plane, 0))
            for whole, block in zip(full, blocks[s])
        ]
    mine_full, other_full, value_full, out_full = full

    t_now = timesteps[0]
    emb = embed(t_now)
    gate = mod_table[2] + emb
    delta = sigma_of(jnp.maximum(t_now - TSTEPS // level_count, 0)) - sigma_of(t_now)
    is_last = level_id == level_count - 1

    def rolled(a):
        parts = [
            lax.dynamic_slice_in_dim(a, ((z - s) % PLANES) * plane, plane, 1)
            for s in range(PLANES)
        ]
        return jnp.concatenate(parts, axis=1)

    normed = normalize(queue.astype(FLOAT), emb, mod_table)
    normed = jnp.concatenate(
        [
            lax.dynamic_slice_in_dim(normed, (tensor_id ^ d) * share, share, 0)
            for d in range(groups)
        ]
    )
    normed = rolled(normed)
    current = lax.dynamic_slice_in_dim(queue, tensor_id * share, share, 0)
    vel_list = []
    for step in range(2):
        if step == 0:
            mine = other = value = 0.0
            for s in ORDER:
                x_part = normed[:, s * plane : (s + 1) * plane]
                mine = mine + dot(x_part, blocks[s][0])
                other = other + dot(x_part, blocks[s][1])
                value = value + dot(x_part, blocks[s][2])
        else:
            mine, other, value = (dot(normed, w) for w in (mine_full, other_full, value_full))
        query = jnp.where(core == 0, mine, other).astype(jnp.bfloat16)
        keys = jnp.where(core == 0, other, mine).astype(jnp.bfloat16)
        attended = attend(query, keys, value.astype(jnp.bfloat16), offsets[0], tensor_id)
        part = dot_t(attended, out_full).astype(jnp.bfloat16)
        proj = part[:share].astype(FLOAT)
        for d in range(1, groups):
            proj = proj + swap(part[d * share : (d + 1) * share], "tensor", d).astype(FLOAT)
        vel = gate * rolled(proj)
        updated = (current.astype(FLOAT) + delta * vel).astype(jnp.bfloat16)
        vel_list.append(vel.astype(jnp.bfloat16))
        moved = lax.ppermute(updated, "level", [(i + 1, i) for i in range(level_count - 1)])
        current = jnp.where(is_last, tail_noise[step], moved)
        if step == 0:
            own = rolled(normalize(current.astype(FLOAT), emb, mod_table))
            normed = jnp.concatenate(
                [own] + [swap(own, "tensor", d) for d in range(1, groups)], axis=0
            )
    return (current, jnp.stack(vel_list))


def solution(mesh):
    in_specs = (
        P("level", None),
        P(None, "tensor", None),
        P("level"),
        P("level"),
        P(),
        P("level", "tensor"),
        P("level", "tensor"),
        P("level", "tensor"),
        P("tensor", "level"),
    )
    out_specs = (P(("level", "tensor"), None), P(None, ("level", "tensor"), None))
    return jax.shard_map(shards, mesh=mesh, in_specs=in_specs, out_specs=out_specs, check_vma=False)
```

```python
import math

import jax
import jax.numpy as jnp
from jax import lax
from jax.experimental import pallas as pl
from jax.experimental.pallas import tpu as pltpu
from jax.sharding import PartitionSpec as P

D = 5120
HD = 128
TSTEPS = 1000
PLANES = 8
PLANE = D // PLANES
HALF = PLANE // 2
QUARTER = PLANE // 4
SHARE = 16
FLOAT = jnp.float32
BF16 = jnp.bfloat16


def sigma_of(t_index):
    unit = t_index.astype(FLOAT) / TSTEPS
    return 5.0 * unit / (1.0 + 4.0 * unit)


def embed(t_index):
    half = D // 2
    freqs = jnp.exp(-math.log(10000.0) * jnp.arange(half, dtype=FLOAT) / half)
    angles = t_index.astype(FLOAT) * freqs
    return jnp.concatenate([jnp.sin(angles), jnp.cos(angles)])


def dot(a, b):
    return jnp.dot(a, b, preferred_element_type=FLOAT)


def dot_t(a, b):
    return lax.dot_general(a, b, (((1,), (1,)), ((), ())), preferred_element_type=FLOAT)


def to_z(block, hops):
    count = lax.axis_size("level")
    return lax.ppermute(block, "level", [(i, (i + 4 * hops) % count) for i in range(count)])


def swap(block, axis, bit):
    return lax.ppermute(block, axis, [(i, i ^ bit) for i in range(lax.axis_size(axis))])


def in_order(own, other, bit, axis=0):
    return jnp.where(
        bit == 0,
        jnp.concatenate([own, other], axis=axis),
        jnp.concatenate([other, own], axis=axis),
    )


def together(*arrays):
    return lax.optimization_barrier(arrays)


def gather_weights(w_query, w_key, w_value, w_out_t, y_hi, core):
    mine = jnp.where(core == 0, w_query, w_key)
    early = in_order(mine, swap(jnp.where(core == 0, w_key, w_query), "level", 1), core)
    mine = jnp.where(core == 0, w_value, w_out_t)
    late = in_order(mine, swap(jnp.where(core == 0, w_out_t, w_value), "level", 1), core)
    wide = late.shape[1]
    early, late = together(early, late)
    full = [jnp.zeros((D, wide), BF16) for _ in range(4)]

    def put(index, block, row):
        full[index] = lax.dynamic_update_slice(full[index], block, (row, 0))

    def early_to_core(block, *places):
        other = swap(block, "level", 1)
        for s, row, start, rows in places:
            put(0, block[start : start + rows], s * PLANE + row)
            put(1, other[start : start + rows], s * PLANE + row)

    def late_to_core(own, got, *planes):
        rows = len(planes) * HALF
        block = in_order(
            own.reshape(len(planes), HALF, wide), got.reshape(len(planes), HALF, wide), y_hi, axis=1
        ).reshape(2 * rows, wide)
        other = swap(block, "level", 1)
        for i, s in enumerate(planes):
            here, there = (a[i * PLANE : (i + 1) * PLANE] for a in (block, other))
            put(2, jnp.where(core == 0, here, there), s * PLANE)
            put(3, jnp.where(core == 0, there, here), s * PLANE)

    crossing, up1, down1 = together(swap(early, "level", 2), to_z(late, 1), to_z(late, -1))
    whole = in_order(early, crossing, y_hi)
    near = jnp.concatenate([late, up1, down1])
    up2, down2, got2 = together(
        to_z(jnp.concatenate([whole, up1]), 1),
        to_z(jnp.concatenate([down1, whole]), -1),
        swap(near, "level", 2),
    )
    early_to_core(whole, (0, 0, 0, PLANE))
    late2 = jnp.concatenate([up2[PLANE:], down2[:HALF]])
    up3, down3, got3 = together(to_z(up2, 1), to_z(down2, -1), swap(late2, "level", 2))
    late_to_core(near, got2, 0, 1, 7)
    early_to_core(up2, (1, 0, 0, PLANE))
    early_to_core(down2, (7, 0, HALF, PLANE))
    late3 = jnp.concatenate([up3[PLANE:], down3[:HALF]])
    up4, down4, got4 = together(
        to_z(up3[: PLANE + QUARTER], 1), to_z(down3[QUARTER:], -1), swap(late3, "level", 2)
    )
    late_to_core(late2, got3, 2, 6)
    early_to_core(up3, (2, 0, 0, PLANE))
    early_to_core(down3, (6, 0, HALF, PLANE))
    late4 = jnp.concatenate([up4[PLANE:], down4[:QUARTER]])
    up5, down5, got5 = together(
        to_z(up4[:HALF], 1), to_z(down4[QUARTER + HALF :], -1), swap(late4, "level", 2)
    )
    late_to_core(late3, got4, 3, 5)
    early_to_core(up4, (3, 0, 0, PLANE))
    early_to_core(down4, (5, 0, QUARTER, PLANE))
    late_to_core(late4, got5, 4)
    early_to_core(jnp.concatenate([up5, down5]), (4, 0, 0, PLANE))
    return full, up1


def project_kernel(info, x, w_own, w_other, w_value, query, key_value, total):
    step = pl.program_id(0)
    part = x[...]
    heads = w_own.shape[1]

    @pl.when(step == 0)
    def _():
        total[...] = jnp.zeros_like(total)

    for i, w in enumerate((w_own, w_other, w_value)):
        total[:, i * heads : (i + 1) * heads] += dot(part, w[...])

    @pl.when(step == pl.num_programs(0) - 1)
    def _():
        own, other = total[:, :heads], total[:, heads : 2 * heads]
        query[...] = jnp.where(info[0] == 0, own, other).astype(BF16)
        key_value[0] = jnp.where(info[0] == 0, other, own).astype(BF16)
        key_value[1] = total[:, 2 * heads :].astype(BF16)


def project(info, rows, own, other, value):
    sec, heads = rows.shape[0], own.shape[1]
    weights = pl.BlockSpec((PLANE, heads), lambda s: (s, 0))
    return pl.pallas_call(
        project_kernel,
        grid=(PLANES,),
        out_shape=(
            jax.ShapeDtypeStruct((sec, heads), BF16),
            jax.ShapeDtypeStruct((2, sec, heads), BF16),
        ),
        in_specs=[
            pl.BlockSpec(memory_space=pltpu.SMEM),
            pl.BlockSpec((sec, PLANE), lambda s: (0, s)),
            weights,
            weights,
            weights,
        ],
        out_specs=(
            pl.BlockSpec((sec, heads), lambda s: (0, 0)),
            pl.BlockSpec((2, sec, heads), lambda s: (0, 0, 0)),
        ),
        scratch_shapes=[pltpu.VMEM((sec, 3 * heads), FLOAT)],
        compiler_params=pltpu.CompilerParams(vmem_limit_bytes=16 * 2**20),
        cost_estimate=pl.CostEstimate(
            flops=6 * sec * D * heads, bytes_accessed=6 * D * heads + 2 * sec * D, transcendentals=0
        ),
    )(info, rows, own, other, value)


def attend_kernel(info, query, low, mid, high, w_out, *refs):
    outs, attended = refs[:8], refs[8]
    offset, tensor_id, first, last = (info[i] for i in range(2, 6))
    sec = query.shape[0]

    @pl.when(pl.program_id(0) == 0)
    def _():
        place = lax.broadcasted_iota(jnp.int32, (1, 3 * sec), 1)
        rows = place ^ (tensor_id * SHARE)
        live = (rows >= offset) & (rows < offset + 2 * sec)
        live = live & ((rows >= sec) | (first == 0)) & ((rows < 2 * sec) | (last == 0))
        for head in range(query.shape[1] // HD):
            cols = slice(head * HD, (head + 1) * HD)
            keys = jnp.concatenate([low[0, :, cols], mid[0, :, cols], high[0, :, cols]], axis=0)
            values = jnp.concatenate([low[1, :, cols], mid[1, :, cols], high[1, :, cols]], axis=0)
            scores = dot_t(query[:, cols], keys) / math.sqrt(HD)
            scores = jnp.where(live, scores, -1e30)
            top = jnp.max(scores, axis=-1, keepdims=True)
            expo = jnp.where(live, jnp.exp(scores - top), 0.0)
            probs = (expo / jnp.sum(expo, axis=-1, keepdims=True)).astype(BF16)
            attended[:, cols] = dot(probs, values).astype(BF16)

    part = dot_t(attended[...], w_out[...]).astype(BF16)
    for d in range(8):
        outs[d][...] = part[d * SHARE : (d + 1) * SHARE]


def attend(info, query, low, mid, high, w_out):
    sec, heads = query.shape
    rows = pl.BlockSpec((2, sec, heads), lambda s: (0, 0, 0))
    return pl.pallas_call(
        attend_kernel,
        grid=(PLANES,),
        out_shape=tuple(jax.ShapeDtypeStruct((SHARE, D), BF16) for _ in range(8)),
        in_specs=[
            pl.BlockSpec(memory_space=pltpu.SMEM),
            pl.BlockSpec((sec, heads), lambda s: (0, 0)),
            rows,
            rows,
            rows,
            pl.BlockSpec((PLANE, heads), lambda s: (s, 0)),
        ],
        out_specs=tuple(pl.BlockSpec((SHARE, PLANE), lambda s: (0, s)) for _ in range(8)),
        scratch_shapes=[pltpu.VMEM((sec, heads), BF16)],
        compiler_params=pltpu.CompilerParams(vmem_limit_bytes=16 * 2**20),
        cost_estimate=pl.CostEstimate(
            flops=2 * sec * D * heads + 12 * sec * sec * heads,
            bytes_accessed=2 * D * heads + 2 * sec * D,
            transcendentals=3 * sec * heads,
        ),
    )(info, query, low, mid, high, w_out)


def normalize(x_float, emb, mod_table):
    mean = jnp.mean(x_float, axis=-1, keepdims=True)
    var = jnp.mean((x_float - mean) ** 2, axis=-1, keepdims=True)
    unit = (x_float - mean) / jnp.sqrt(var + 1e-06)
    return (unit * (1.0 + mod_table[1] + 0.5 * emb) + mod_table[0] + emb).astype(BF16)


def shards(queue, tail_noise, timesteps, offsets, mod_table, w_query, w_key, w_value, w_out):
    level_id = lax.axis_index("level")
    level_count = lax.axis_size("level")
    tensor_id = lax.axis_index("tensor")
    groups = lax.axis_size("tensor")
    z, y_hi, core = level_id // 4, (level_id // 2) % 2, level_id % 2
    is_last = level_id == level_count - 1
    info = jnp.stack(
        [
            core,
            y_hi,
            offsets[0],
            tensor_id,
            (level_id == 0).astype(jnp.int32),
            is_last.astype(jnp.int32),
        ]
    )
    up = [(i, i + 1) for i in range(level_count - 1)]
    down = [(i + 1, i) for i in range(level_count - 1)]

    (own, other, value, out_t), first_come = gather_weights(w_query, w_key, w_value, w_out.T, y_hi, core)
    queue, _ = together(queue, first_come)

    t_now = timesteps[0]
    emb = embed(t_now)
    gate = mod_table[2] + emb
    delta = sigma_of(jnp.maximum(t_now - TSTEPS // level_count, 0)) - sigma_of(t_now)

    def rolled(a):
        parts = [
            lax.dynamic_slice_in_dim(a, ((z - s) % PLANES) * PLANE, PLANE, 1)
            for s in range(PLANES)
        ]
        return jnp.concatenate(parts, axis=1)

    normed = rolled(normalize(queue.astype(FLOAT), emb, mod_table))
    rows = jnp.concatenate(
        [
            lax.dynamic_slice_in_dim(normed, (tensor_id ^ d) * SHARE, SHARE, 0)
            for d in range(groups)
        ]
    )
    current = lax.dynamic_slice_in_dim(queue, tensor_id * SHARE, SHARE, 0)
    vel_list = []
    for step in range(2):
        query, mid = project(info, rows, own, other, value)
        low, high = together(lax.ppermute(mid, "level", up), lax.ppermute(mid, "level", down))
        parts = attend(info, query, low, mid, high, out_t)
        arrived = together(*[swap(parts[d], "tensor", d) for d in range(1, groups)])
        proj = parts[0].astype(FLOAT)
        for part in arrived:
            proj = proj + part.astype(FLOAT)
        vel = gate * rolled(proj)
        updated = (current.astype(FLOAT) + delta * vel).astype(BF16)
        vel_list.append(vel.astype(BF16))
        current = jnp.where(is_last, tail_noise[step], lax.ppermute(updated, "level", down))
        if step == 0:
            mine = rolled(normalize(current.astype(FLOAT), emb, mod_table))
            arrived = together(*[swap(mine, "tensor", d) for d in range(1, groups)])
            rows = jnp.concatenate([mine, *arrived])
    return (current, jnp.stack(vel_list))


def solution(mesh):
    in_specs = (
        P("level", None),
        P(None, "tensor", None),
        P("level"),
        P("level"),
        P(),
        P("level", "tensor"),
        P("level", "tensor"),
        P("level", "tensor"),
        P("tensor", "level"),
    )
    out_specs = (P(("level", "tensor"), None), P(None, ("level", "tensor"), None))
    return jax.shard_map(shards, mesh=mesh, in_specs=in_specs, out_specs=out_specs, check_vma=False)
```

```python
import math

import jax
import jax.numpy as jnp
from jax import lax
from jax.experimental import pallas as pl
from jax.experimental.pallas import tpu as pltpu
from jax.sharding import PartitionSpec as P

D = 5120
HD = 128
TSTEPS = 1000
PLANES = 8
PLANE = D // PLANES
HALF = PLANE // 2
QUARTER = PLANE // 4
SHARE = 16
SENDS = (1, 5, 4, 7, 3, 6, 2)
RADIX = 32
FLOAT = jnp.float32
BF16 = jnp.bfloat16


def sigma_of(t_index):
    unit = t_index.astype(FLOAT) / TSTEPS
    return 5.0 * unit / (1.0 + 4.0 * unit)


def embed(t_index):
    half = D // 2
    freqs = jnp.exp(-math.log(10000.0) * jnp.arange(half, dtype=FLOAT) / half)
    angles = t_index.astype(FLOAT) * freqs
    return jnp.concatenate([jnp.sin(angles), jnp.cos(angles)])


def dot(a, b):
    return jnp.dot(a, b, preferred_element_type=FLOAT)


def dot_t(a, b):
    return lax.dot_general(a, b, (((1,), (1,)), ((), ())), preferred_element_type=FLOAT)


def to_z(block, hops):
    count = lax.axis_size("level")
    return lax.ppermute(block, "level", [(i, (i + 4 * hops) % count) for i in range(count)])


def swap(block, axis, bit):
    return lax.ppermute(block, axis, [(i, i ^ bit) for i in range(lax.axis_size(axis))])


def moved(block, distance):
    count = lax.axis_size("level")
    return lax.ppermute(block, "level", [(i, (i + distance) % count) for i in range(count)])


def in_order(own, other, bit, axis=0):
    return jnp.where(
        bit == 0,
        jnp.concatenate([own, other], axis=axis),
        jnp.concatenate([other, own], axis=axis),
    )


def together(*arrays):
    return lax.optimization_barrier(arrays)


def gather_weights(w_query, w_key, w_value, w_out_t, y_hi, core):
    mine = jnp.where(core == 0, w_query, w_key)
    early = in_order(mine, swap(jnp.where(core == 0, w_key, w_query), "level", 1), core)
    mine = jnp.where(core == 0, w_value, w_out_t)
    late = in_order(mine, swap(jnp.where(core == 0, w_out_t, w_value), "level", 1), core)
    wide = late.shape[1]
    early, late = together(early, late)
    full = [jnp.zeros((D, wide), BF16) for _ in range(4)]

    def put(index, block, row):
        full[index] = lax.dynamic_update_slice(full[index], block, (row, 0))

    def early_to_core(block, *places):
        other = swap(block, "level", 1)
        for s, row, start, rows in places:
            put(0, block[start : start + rows], s * PLANE + row)
            put(1, other[start : start + rows], s * PLANE + row)

    def late_to_core(own, got, *planes):
        rows = len(planes) * HALF
        block = in_order(
            own.reshape(len(planes), HALF, wide), got.reshape(len(planes), HALF, wide), y_hi, axis=1
        ).reshape(2 * rows, wide)
        other = swap(block, "level", 1)
        for i, s in enumerate(planes):
            here, there = (a[i * PLANE : (i + 1) * PLANE] for a in (block, other))
            put(2, jnp.where(core == 0, here, there), s * PLANE)
            put(3, jnp.where(core == 0, there, here), s * PLANE)

    crossing, up1, down1 = together(swap(early, "level", 2), to_z(late, 1), to_z(late, -1))
    whole = in_order(early, crossing, y_hi)
    near = jnp.concatenate([late, up1, down1])
    up2, down2, got2 = together(
        to_z(jnp.concatenate([whole, up1]), 1),
        to_z(jnp.concatenate([down1, whole]), -1),
        swap(near, "level", 2),
    )
    early_to_core(whole, (0, 0, 0, PLANE))
    late2 = jnp.concatenate([up2[PLANE:], down2[:HALF]])
    up3, down3, got3 = together(to_z(up2, 1), to_z(down2, -1), swap(late2, "level", 2))
    late_to_core(near, got2, 0, 1, 7)
    early_to_core(up2, (1, 0, 0, PLANE))
    early_to_core(down2, (7, 0, HALF, PLANE))
    late3 = jnp.concatenate([up3[PLANE:], down3[:HALF]])
    up4, down4, got4 = together(
        to_z(up3[: PLANE + QUARTER], 1), to_z(down3[QUARTER:], -1), swap(late3, "level", 2)
    )
    late_to_core(late2, got3, 2, 6)
    early_to_core(up3, (2, 0, 0, PLANE))
    early_to_core(down3, (6, 0, HALF, PLANE))
    late4 = jnp.concatenate([up4[PLANE:], down4[:QUARTER]])
    up5, down5, got5 = together(
        to_z(up4[:HALF], 1), to_z(down4[QUARTER + HALF :], -1), swap(late4, "level", 2)
    )
    late_to_core(late3, got4, 3, 5)
    early_to_core(up4, (3, 0, 0, PLANE))
    early_to_core(down4, (5, 0, QUARTER, PLANE))
    late_to_core(late4, got5, 4)
    early_to_core(jnp.concatenate([up5, down5]), (4, 0, 0, PLANE))
    return full, up1


def project_kernel(info, x, w_own, w_other, w_value, query, key_value, total):
    step = pl.program_id(0)
    part = x[...]
    heads = w_own.shape[1]

    @pl.when(step == 0)
    def _():
        total[...] = jnp.zeros_like(total)

    for i, w in enumerate((w_own, w_other, w_value)):
        total[:, i * heads : (i + 1) * heads] += dot(part, w[...])

    @pl.when(step == pl.num_programs(0) - 1)
    def _():
        own, other = total[:, :heads], total[:, heads : 2 * heads]
        query[...] = jnp.where(info[0] == 0, own, other).astype(BF16)
        sec = total.shape[0]
        key_value[0, :sec] = jnp.where(info[0] == 0, other, own).astype(BF16)
        key_value[1, :sec] = total[:, 2 * heads :].astype(BF16)
        shape = (SHARE, heads)
        high, offset = info[1] // RADIX, info[2]
        left = lax.broadcasted_iota(jnp.int32, shape, 1) < HD
        key_value[0, sec:] = jnp.where(left, high, offset).astype(FLOAT).astype(BF16)
        key_value[1, sec:] = jnp.full(shape, info[1] - high * RADIX).astype(FLOAT).astype(BF16)


def project(info, rows, own, other, value):
    sec, heads = rows.shape[0], own.shape[1]
    weights = pl.BlockSpec((PLANE, heads), lambda s: (s, 0))
    return pl.pallas_call(
        project_kernel,
        grid=(PLANES,),
        out_shape=(
            jax.ShapeDtypeStruct((sec, heads), BF16),
            jax.ShapeDtypeStruct((2, sec + SHARE, heads), BF16),
        ),
        in_specs=[
            pl.BlockSpec(memory_space=pltpu.SMEM),
            pl.BlockSpec((sec, PLANE), lambda s: (0, s)),
            weights,
            weights,
            weights,
        ],
        out_specs=(
            pl.BlockSpec((sec, heads), lambda s: (0, 0)),
            pl.BlockSpec((2, sec + SHARE, heads), lambda s: (0, 0, 0)),
        ),
        scratch_shapes=[pltpu.VMEM((sec, 3 * heads), FLOAT)],
        compiler_params=pltpu.CompilerParams(vmem_limit_bytes=16 * 2**20),
        cost_estimate=pl.CostEstimate(
            flops=6 * sec * D * heads, bytes_accessed=6 * D * heads + 2 * sec * D, transcendentals=0
        ),
    )(info, rows, own, other, value)


def attend_kernel(info, query, low, mid, high, w_out, *refs):
    outs, attended = refs[:8], refs[8]
    offset, tensor_id, first, last = (info[i] for i in range(2, 6))
    sec = query.shape[0]

    @pl.when(pl.program_id(0) == 0)
    def _():
        place = lax.broadcasted_iota(jnp.int32, (1, 3 * sec), 1)
        rows = place ^ (tensor_id * SHARE)
        live = (rows >= offset) & (rows < offset + 2 * sec)
        live = live & ((rows >= sec) | (first == 0)) & ((rows < 2 * sec) | (last == 0))
        for head in range(query.shape[1] // HD):
            cols = slice(head * HD, (head + 1) * HD)
            keys = jnp.concatenate([a[0, :sec, cols] for a in (low, mid, high)], axis=0)
            values = jnp.concatenate([a[1, :sec, cols] for a in (low, mid, high)], axis=0)
            scores = dot_t(query[:, cols], keys) / math.sqrt(HD)
            scores = jnp.where(live, scores, -1e30)
            top = jnp.max(scores, axis=-1, keepdims=True)
            expo = jnp.where(live, jnp.exp(scores - top), 0.0)
            probs = (expo / jnp.sum(expo, axis=-1, keepdims=True)).astype(BF16)
            attended[:, cols] = dot(probs, values).astype(BF16)

    part = dot_t(attended[...], w_out[...]).astype(BF16)
    for d in range(8):
        outs[d][...] = part[d * SHARE : (d + 1) * SHARE]


def attend(info, query, low, mid, high, w_out):
    sec, heads = query.shape
    rows = pl.BlockSpec(low.shape, lambda s: (0, 0, 0))
    return pl.pallas_call(
        attend_kernel,
        grid=(PLANES,),
        out_shape=tuple(jax.ShapeDtypeStruct((SHARE, D), BF16) for _ in range(8)),
        in_specs=[
            pl.BlockSpec(memory_space=pltpu.SMEM),
            pl.BlockSpec((sec, heads), lambda s: (0, 0)),
            rows,
            rows,
            rows,
            pl.BlockSpec((PLANE, heads), lambda s: (s, 0)),
        ],
        out_specs=tuple(pl.BlockSpec((SHARE, PLANE), lambda s: (0, s)) for _ in range(8)),
        scratch_shapes=[pltpu.VMEM((sec, heads), BF16)],
        compiler_params=pltpu.CompilerParams(vmem_limit_bytes=16 * 2**20),
        cost_estimate=pl.CostEstimate(
            flops=2 * sec * D * heads + 12 * sec * sec * heads,
            bytes_accessed=2 * D * heads + 2 * sec * D,
            transcendentals=3 * sec * heads,
        ),
    )(info, query, low, mid, high, w_out)


def normalize(x_float, emb, mod_table):
    mean = jnp.mean(x_float, axis=-1, keepdims=True)
    var = jnp.mean((x_float - mean) ** 2, axis=-1, keepdims=True)
    unit = (x_float - mean) / jnp.sqrt(var + 1e-06)
    return (unit * (1.0 + mod_table[1] + 0.5 * emb) + mod_table[0] + emb).astype(BF16)


def exchange(blocks):
    got = together(*[swap(blocks[d], "tensor", d) for d in SENDS])
    return [got[SENDS.index(d)] for d in range(1, 8)]


def shards(queue, tail_noise, timesteps, offsets, mod_table, w_query, w_key, w_value, w_out):
    level_id = lax.axis_index("level")
    level_count = lax.axis_size("level")
    tensor_id = lax.axis_index("tensor")
    groups = lax.axis_size("tensor")
    z, y_hi, core = level_id // 4, (level_id // 2) % 2, level_id % 2

    (own, other, value, out_t), first_come = gather_weights(
        w_query, w_key, w_value, w_out.T, y_hi, core
    )
    queue, timesteps, offsets, _ = together(queue, timesteps, offsets, first_come)
    t_now, offset = timesteps[0], offsets[0]
    emb = embed(t_now)

    def rolled(a):
        parts = [
            lax.dynamic_slice_in_dim(a, ((z - s) % PLANES) * PLANE, PLANE, 1)
            for s in range(PLANES)
        ]
        return jnp.concatenate(parts, axis=1)

    normed = rolled(normalize(queue.astype(FLOAT), emb, mod_table))
    rows = jnp.concatenate(
        [
            lax.dynamic_slice_in_dim(normed, (tensor_id ^ d) * SHARE, SHARE, 0)
            for d in range(groups)
        ]
    )
    current = lax.dynamic_slice_in_dim(queue, tensor_id * SHARE, SHARE, 0)
    vel_list = []
    for step in range(2):
        section = (level_id - step) % level_count
        ends = [(section == end).astype(jnp.int32) for end in (0, level_count - 1)]
        info = jnp.stack([core, t_now, offset, tensor_id, *ends])
        gate = mod_table[2] + emb
        delta = sigma_of(jnp.maximum(t_now - TSTEPS // level_count, 0)) - sigma_of(t_now)

        query, mid = project(info, rows, own, other, value)
        low, high = together(moved(mid, 1), moved(mid, -1))
        parts = attend(info, query, low, mid, high, out_t)
        proj = parts[0].astype(FLOAT)
        for part in exchange(parts):
            proj = proj + part.astype(FLOAT)
        vel = gate * rolled(proj)
        updated = (current.astype(FLOAT) + delta * vel).astype(BF16)
        vel_list.append(vel.astype(BF16))
        if step == 0:
            t_now = (low[0, -1, 0].astype(FLOAT) * RADIX + low[1, -1, 0].astype(FLOAT)).astype(jnp.int32)
            offset = low[0, -1, -1].astype(jnp.int32)
            emb = embed(t_now)
            current = jnp.where(level_id == 0, tail_noise[0], updated)
            mine = rolled(normalize(current.astype(FLOAT), emb, mod_table))
            rows = jnp.concatenate([mine, *exchange([mine] * groups)])
    final, vel_list[1] = together(moved(updated, -2), moved(vel_list[1], -1))
    final = jnp.where(level_id == level_count - 1, tail_noise[1], final)
    return (final, jnp.stack(vel_list))


def solution(mesh):
    in_specs = (
        P("level", None),
        P(None, "tensor", None),
        P("level"),
        P("level"),
        P(),
        P("level", "tensor"),
        P("level", "tensor"),
        P("level", "tensor"),
        P("tensor", "level"),
    )
    out_specs = (P(("level", "tensor"), None), P(None, ("level", "tensor"), None))
    return jax.shard_map(shards, mesh=mesh, in_specs=in_specs, out_specs=out_specs, check_vma=False)
```

```python
import math

import jax
import jax.numpy as jnp
from jax import lax
from jax.experimental import pallas as pl
from jax.experimental.pallas import tpu as pltpu
from jax.sharding import PartitionSpec as P

D = 5120
HD = 128
TSTEPS = 1000
PLANES = 8
PLANE = D // PLANES
HALF = PLANE // 2
QUARTER = PLANE // 4
SHARE = 16
FAR = 4
SENDS = (1, 5, 4, 7, 3, 6, 2)
RADIX = 32
FLOAT = jnp.float32
BF16 = jnp.bfloat16


def sigma_of(t_index):
    unit = t_index.astype(FLOAT) / TSTEPS
    return 5.0 * unit / (1.0 + 4.0 * unit)


def embed(t_index):
    half = D // 2
    freqs = jnp.exp(-math.log(10000.0) * jnp.arange(half, dtype=FLOAT) / half)
    angles = t_index.astype(FLOAT) * freqs
    return jnp.concatenate([jnp.sin(angles), jnp.cos(angles)])


def dot(a, b):
    return jnp.dot(a, b, preferred_element_type=FLOAT)


def dot_t(a, b):
    return lax.dot_general(a, b, (((1,), (1,)), ((), ())), preferred_element_type=FLOAT)


def to_z(block, hops):
    count = lax.axis_size("level")
    return lax.ppermute(block, "level", [(i, (i + 4 * hops) % count) for i in range(count)])


def swap(block, axis, bit):
    return lax.ppermute(block, axis, [(i, i ^ bit) for i in range(lax.axis_size(axis))])


def moved(block, distance):
    count = lax.axis_size("level")
    return lax.ppermute(block, "level", [(i, (i + distance) % count) for i in range(count)])


def in_order(own, other, bit, axis=0):
    return jnp.where(
        bit == 0,
        jnp.concatenate([own, other], axis=axis),
        jnp.concatenate([other, own], axis=axis),
    )


def together(*arrays):
    return lax.optimization_barrier(arrays)


def gather_weights(w_query, w_key, w_value, w_out_t, y_hi, core):
    mine = jnp.where(core == 0, w_query, w_key)
    early = in_order(mine, swap(jnp.where(core == 0, w_key, w_query), "level", 1), core)
    mine = jnp.where(core == 0, w_value, w_out_t)
    late = in_order(mine, swap(jnp.where(core == 0, w_out_t, w_value), "level", 1), core)
    wide = late.shape[1]
    early, late = together(early, late)
    near_planes = D - PLANE
    full = [jnp.zeros((near_planes, wide), BF16) for _ in range(4)]
    far = [None] * 4

    def put(index, block, row):
        if row == FAR * PLANE:
            far[index] = block
        else:
            row = row - PLANE if row > FAR * PLANE else row
            full[index] = lax.dynamic_update_slice(full[index], block, (row, 0))

    def early_to_core(block, *places):
        other = swap(block, "level", 1)
        for s, row, start, rows in places:
            put(0, block[start : start + rows], s * PLANE + row)
            put(1, other[start : start + rows], s * PLANE + row)

    def early_pair_to_core(up, down, s_up, s_down):
        places = ((s_up, 0, 0, PLANE), (s_down, 0, PLANE, PLANE))
        early_to_core(jnp.concatenate([up, down]), *places)

    def late_to_core(own, got, *planes):
        rows = len(planes) * HALF
        block = in_order(
            own.reshape(len(planes), HALF, wide), got.reshape(len(planes), HALF, wide), y_hi, axis=1
        ).reshape(2 * rows, wide)
        other = swap(block, "level", 1)
        for i, s in enumerate(planes):
            here, there = (a[i * PLANE : (i + 1) * PLANE] for a in (block, other))
            put(2, jnp.where(core == 0, here, there), s * PLANE)
            put(3, jnp.where(core == 0, there, here), s * PLANE)

    crossing, up1, down1 = together(swap(early, "level", 2), to_z(late, 1), to_z(late, -1))
    whole = in_order(early, crossing, y_hi)
    near = jnp.concatenate([late, up1, down1])
    up2, down2, got2 = together(
        to_z(jnp.concatenate([whole, up1]), 1),
        to_z(jnp.concatenate([down1, whole]), -1),
        swap(near, "level", 2),
    )
    early_to_core(whole, (0, 0, 0, PLANE))
    late2 = jnp.concatenate([up2[PLANE:], down2[:HALF]])
    up3, down3, got3 = together(to_z(up2, 1), to_z(down2, -1), swap(late2, "level", 2))
    late_to_core(near, got2, 0, 1, 7)
    early_pair_to_core(up2[:PLANE], down2[HALF:], 1, 7)
    late3 = jnp.concatenate([up3[PLANE:], down3[:HALF]])
    up4, down4, got4 = together(
        to_z(up3[: PLANE + QUARTER], 1), to_z(down3[QUARTER:], -1), swap(late3, "level", 2)
    )
    late_to_core(late2, got3, 2, 6)
    early_pair_to_core(up3[:PLANE], down3[HALF:], 2, 6)
    late4 = jnp.concatenate([up4[PLANE:], down4[:QUARTER]])
    up5, down5 = together(
        to_z(jnp.concatenate([up4[:HALF], got4[:QUARTER]]), 1),
        to_z(jnp.concatenate([got4[HALF + QUARTER :], down4[QUARTER + HALF :]]), -1),
    )
    late_to_core(late3, got4, 3, 5)
    early_pair_to_core(up4[:PLANE], down4[QUARTER:], 3, 5)
    early_to_core(jnp.concatenate([up5[:HALF], down5[QUARTER:]]), (FAR, 0, 0, PLANE))
    late_to_core(late4, jnp.concatenate([up5[HALF:], down5[:QUARTER]]), FAR)
    return full, far, up1


def near_kernel(x, w_own, w_other, w_value, total):
    heads = w_own.shape[1]

    @pl.when(pl.program_id(0) == 0)
    def _():
        total[...] = jnp.zeros_like(total)

    part = x[...]
    for i, w in enumerate((w_own, w_other, w_value)):
        total[:, i * heads : (i + 1) * heads] += dot(part, w[...])


def far_kernel(info, x, w_own, w_other, w_value, total, query, key_value):
    sec, heads = query.shape
    part = x[...]
    own, other, value = (
        total[:, i * heads : (i + 1) * heads] + dot(part, w[...])
        for i, w in enumerate((w_own, w_other, w_value))
    )
    query[...] = jnp.where(info[0] == 0, own, other).astype(BF16)
    key_value[0, :sec] = jnp.where(info[0] == 0, other, own).astype(BF16)
    key_value[1, :sec] = value.astype(BF16)
    shape = (SHARE, heads)
    high, offset = info[1] // RADIX, info[2]
    left = lax.broadcasted_iota(jnp.int32, shape, 1) < HD
    key_value[0, sec:] = jnp.where(left, high, offset).astype(FLOAT).astype(BF16)
    key_value[1, sec:] = jnp.full(shape, info[1] - high * RADIX).astype(FLOAT).astype(BF16)


def project(info, rows, full, far):
    sec, heads = rows.shape[0], far[0].shape[1]
    weights = pl.BlockSpec((PLANE, heads), lambda i: (i, 0))
    sums = jax.ShapeDtypeStruct((sec, 3 * heads), FLOAT)
    total = pl.pallas_call(
        near_kernel,
        grid=(PLANES - 1,),
        out_shape=sums,
        in_specs=[
            pl.BlockSpec((sec, PLANE), lambda i: (0, jnp.where(i < FAR, i, i + 1))),
            weights,
            weights,
            weights,
        ],
        out_specs=pl.BlockSpec(sums.shape, lambda i: (0, 0)),
        compiler_params=pltpu.CompilerParams(vmem_limit_bytes=16 * 2**20),
        cost_estimate=pl.CostEstimate(
            flops=6 * sec * (D - PLANE) * heads,
            bytes_accessed=6 * (D - PLANE) * heads + 2 * sec * D,
            transcendentals=0,
        ),
    )(rows, *full[:3])
    whole = pl.BlockSpec((PLANE, heads), lambda i: (0, 0))
    return pl.pallas_call(
        far_kernel,
        grid=(1,),
        out_shape=(
            jax.ShapeDtypeStruct((sec, heads), BF16),
            jax.ShapeDtypeStruct((2, sec + SHARE, heads), BF16),
        ),
        in_specs=[
            pl.BlockSpec(memory_space=pltpu.SMEM),
            pl.BlockSpec((sec, PLANE), lambda i: (0, FAR)),
            whole,
            whole,
            whole,
            pl.BlockSpec(sums.shape, lambda i: (0, 0)),
        ],
        out_specs=(
            pl.BlockSpec((sec, heads), lambda i: (0, 0)),
            pl.BlockSpec((2, sec + SHARE, heads), lambda i: (0, 0, 0)),
        ),
        compiler_params=pltpu.CompilerParams(vmem_limit_bytes=16 * 2**20),
        cost_estimate=pl.CostEstimate(
            flops=6 * sec * PLANE * heads, bytes_accessed=6 * PLANE * heads, transcendentals=0
        ),
    )(info, rows, *far[:3], total)


def attend_kernel(info, query, low, mid, high, w_near, w_far, *refs):
    outs, attended = refs[:8], refs[8]
    offset, tensor_id, first, last = (info[i] for i in range(2, 6))
    sec = query.shape[0]

    @pl.when(pl.program_id(0) == 0)
    def _():
        place = lax.broadcasted_iota(jnp.int32, (1, 3 * sec), 1)
        rows = place ^ (tensor_id * SHARE)
        live = (rows >= offset) & (rows < offset + 2 * sec)
        live = live & ((rows >= sec) | (first == 0)) & ((rows < 2 * sec) | (last == 0))
        for head in range(query.shape[1] // HD):
            cols = slice(head * HD, (head + 1) * HD)
            keys = jnp.concatenate([a[0, :sec, cols] for a in (low, mid, high)], axis=0)
            values = jnp.concatenate([a[1, :sec, cols] for a in (low, mid, high)], axis=0)
            scores = dot_t(query[:, cols], keys) / math.sqrt(HD)
            scores = jnp.where(live, scores, -1e30)
            top = jnp.max(scores, axis=-1, keepdims=True)
            expo = jnp.where(live, jnp.exp(scores - top), 0.0)
            probs = (expo / jnp.sum(expo, axis=-1, keepdims=True)).astype(BF16)
            attended[:, cols] = dot(probs, values).astype(BF16)

    def write(w_out):
        part = dot_t(attended[...], w_out[...]).astype(BF16)
        for d in range(8):
            outs[d][...] = part[d * SHARE : (d + 1) * SHARE]

    @pl.when(pl.program_id(0) < PLANES - 1)
    def _():
        write(w_near)

    @pl.when(pl.program_id(0) == PLANES - 1)
    def _():
        write(w_far)


def attend(info, query, low, mid, high, w_near, w_far):
    sec, heads = query.shape
    rows = pl.BlockSpec(low.shape, lambda s: (0, 0, 0))
    return pl.pallas_call(
        attend_kernel,
        grid=(PLANES,),
        out_shape=tuple(jax.ShapeDtypeStruct((SHARE, D), BF16) for _ in range(8)),
        in_specs=[
            pl.BlockSpec(memory_space=pltpu.SMEM),
            pl.BlockSpec((sec, heads), lambda s: (0, 0)),
            rows,
            rows,
            rows,
            pl.BlockSpec((PLANE, heads), lambda s: (jnp.minimum(s, PLANES - 2), 0)),
            pl.BlockSpec((PLANE, heads), lambda s: (0, 0)),
        ],
        out_specs=tuple(
            pl.BlockSpec(
                (SHARE, PLANE),
                lambda s: (0, jnp.where(s < FAR, s, jnp.where(s == PLANES - 1, FAR, s + 1))),
            )
            for _ in range(8)
        ),
        scratch_shapes=[pltpu.VMEM((sec, heads), BF16)],
        compiler_params=pltpu.CompilerParams(vmem_limit_bytes=16 * 2**20),
        cost_estimate=pl.CostEstimate(
            flops=2 * sec * D * heads + 12 * sec * sec * heads,
            bytes_accessed=2 * D * heads + 2 * sec * D,
            transcendentals=3 * sec * heads,
        ),
    )(info, query, low, mid, high, w_near, w_far)


def normalize(x_float, emb, mod_table):
    mean = jnp.mean(x_float, axis=-1, keepdims=True)
    var = jnp.mean((x_float - mean) ** 2, axis=-1, keepdims=True)
    unit = (x_float - mean) / jnp.sqrt(var + 1e-06)
    return (unit * (1.0 + mod_table[1] + 0.5 * emb) + mod_table[0] + emb).astype(BF16)


def exchange(blocks):
    got = together(*[swap(blocks[d], "tensor", d) for d in SENDS])
    return [got[SENDS.index(d)] for d in range(1, 8)]


def shards(queue, tail_noise, timesteps, offsets, mod_table, w_query, w_key, w_value, w_out):
    level_id = lax.axis_index("level")
    level_count = lax.axis_size("level")
    tensor_id = lax.axis_index("tensor")
    groups = lax.axis_size("tensor")
    z, y_hi, core = level_id // 4, (level_id // 2) % 2, level_id % 2

    full, far, first_come = gather_weights(
        w_query, w_key, w_value, w_out.T, y_hi, core
    )
    queue, timesteps, offsets, _ = together(queue, timesteps, offsets, first_come)
    t_now, offset = timesteps[0], offsets[0]
    emb = embed(t_now)

    def rolled(a):
        parts = [
            lax.dynamic_slice_in_dim(a, ((z - s) % PLANES) * PLANE, PLANE, 1)
            for s in range(PLANES)
        ]
        return jnp.concatenate(parts, axis=1)

    normed = rolled(normalize(queue.astype(FLOAT), emb, mod_table))
    rows = jnp.concatenate(
        [
            lax.dynamic_slice_in_dim(normed, (tensor_id ^ d) * SHARE, SHARE, 0)
            for d in range(groups)
        ]
    )
    current = lax.dynamic_slice_in_dim(queue, tensor_id * SHARE, SHARE, 0)
    vel_list = []
    for step in range(2):
        section = (level_id - step) % level_count
        ends = [(section == end).astype(jnp.int32) for end in (0, level_count - 1)]
        info = jnp.stack([core, t_now, offset, tensor_id, *ends])
        gate = mod_table[2] + emb
        delta = sigma_of(jnp.maximum(t_now - TSTEPS // level_count, 0)) - sigma_of(t_now)

        query, mid = project(info, rows, full, far)
        low, high = together(moved(mid, 1), moved(mid, -1))
        parts = attend(info, query, low, mid, high, full[3], far[3])
        proj = parts[0].astype(FLOAT)
        for part in exchange(parts):
            proj = proj + part.astype(FLOAT)
        vel = gate * rolled(proj)
        updated = (current.astype(FLOAT) + delta * vel).astype(BF16)
        vel_list.append(vel.astype(BF16))
        if step == 0:
            low, _ = together(low, parts[0])
            t_now = (low[0, -1, 0].astype(FLOAT) * RADIX + low[1, -1, 0].astype(FLOAT)).astype(jnp.int32)
            offset = low[0, -1, -1].astype(jnp.int32)
            emb = embed(t_now)
            current = jnp.where(level_id == 0, tail_noise[0], updated)
            mine = rolled(normalize(current.astype(FLOAT), emb, mod_table))
            rows = jnp.concatenate([mine, *exchange([mine] * groups)])
    final, vel_list[1] = together(moved(updated, -2), moved(vel_list[1], -1))
    final = jnp.where(level_id == level_count - 1, tail_noise[1], final)
    return (final, jnp.stack(vel_list))


def solution(mesh):
    in_specs = (
        P("level", None),
        P(None, "tensor", None),
        P("level"),
        P("level"),
        P(),
        P("level", "tensor"),
        P("level", "tensor"),
        P("level", "tensor"),
        P("tensor", "level"),
    )
    out_specs = (P(("level", "tensor"), None), P(None, ("level", "tensor"), None))
    return jax.shard_map(shards, mesh=mesh, in_specs=in_specs, out_specs=out_specs, check_vma=False)
```

```python
import math

import jax
import jax.numpy as jnp
from jax import lax
from jax.experimental import pallas as pl
from jax.experimental.pallas import tpu as pltpu
from jax.sharding import PartitionSpec as P

D = 5120
HD = 128
TSTEPS = 1000
PLANES = 8
PLANE = D // PLANES
HALF = PLANE // 2
QUARTER = PLANE // 4
SHARE = 16
FAR = 4
SENDS = (1, 5, 4, 7, 3, 6, 2)
RADIX = 32
FLOAT = jnp.float32
BF16 = jnp.bfloat16


def sigma_of(t_index):
    unit = t_index.astype(FLOAT) / TSTEPS
    return 5.0 * unit / (1.0 + 4.0 * unit)


def embed(t_index):
    half = D // 2
    freqs = jnp.exp(-math.log(10000.0) * jnp.arange(half, dtype=FLOAT) / half)
    angles = t_index.astype(FLOAT) * freqs
    return jnp.concatenate([jnp.sin(angles), jnp.cos(angles)])


def dot(a, b):
    return jnp.dot(a, b, preferred_element_type=FLOAT)


def dot_t(a, b):
    return lax.dot_general(a, b, (((1,), (1,)), ((), ())), preferred_element_type=FLOAT)


def to_z(block, hops):
    count = lax.axis_size("level")
    return lax.ppermute(block, "level", [(i, (i + 4 * hops) % count) for i in range(count)])


def swap(block, axis, bit):
    return lax.ppermute(block, axis, [(i, i ^ bit) for i in range(lax.axis_size(axis))])


def moved(block, distance):
    count = lax.axis_size("level")
    return lax.ppermute(block, "level", [(i, (i + distance) % count) for i in range(count)])


def in_order(own, other, bit, axis=0):
    return jnp.where(
        bit == 0,
        jnp.concatenate([own, other], axis=axis),
        jnp.concatenate([other, own], axis=axis),
    )


def together(*arrays):
    return lax.optimization_barrier(arrays)


def gather_weights(w_query, w_key, w_value, w_out_t, y_hi, core):
    mine = jnp.where(core == 0, w_query, w_key)
    early = in_order(mine, swap(jnp.where(core == 0, w_key, w_query), "level", 1), core)
    mine = jnp.where(core == 0, w_value, w_out_t)
    late = in_order(mine, swap(jnp.where(core == 0, w_out_t, w_value), "level", 1), core)
    wide = late.shape[1]
    early, late = together(early, late)
    near_planes = D - PLANE
    full = [jnp.zeros((near_planes, wide), BF16) for _ in range(4)]
    far = [None] * 4

    def put(index, block, row):
        if row == FAR * PLANE:
            far[index] = block
        else:
            row = row - PLANE if row > FAR * PLANE else row
            full[index] = lax.dynamic_update_slice(full[index], block, (row, 0))

    def early_to_core(block, *places):
        other = swap(block, "level", 1)
        for s, row, start, rows in places:
            put(0, block[start : start + rows], s * PLANE + row)
            put(1, other[start : start + rows], s * PLANE + row)

    def early_pair_to_core(up, down, s_up, s_down):
        places = ((s_up, 0, 0, PLANE), (s_down, 0, PLANE, PLANE))
        early_to_core(jnp.concatenate([up, down]), *places)

    def late_to_core(own, got, *planes):
        rows = len(planes) * HALF
        block = in_order(
            own.reshape(len(planes), HALF, wide), got.reshape(len(planes), HALF, wide), y_hi, axis=1
        ).reshape(2 * rows, wide)
        other = swap(block, "level", 1)
        for i, s in enumerate(planes):
            here, there = (a[i * PLANE : (i + 1) * PLANE] for a in (block, other))
            put(2, jnp.where(core == 0, here, there), s * PLANE)
            put(3, jnp.where(core == 0, there, here), s * PLANE)

    crossing, up1, down1 = together(swap(early, "level", 2), to_z(late, 1), to_z(late, -1))
    whole = in_order(early, crossing, y_hi)
    near = jnp.concatenate([late, up1, down1])
    up2, down2, got2 = together(
        to_z(jnp.concatenate([whole, up1]), 1),
        to_z(jnp.concatenate([down1, whole]), -1),
        swap(near, "level", 2),
    )
    early_to_core(whole, (0, 0, 0, PLANE))
    late2 = jnp.concatenate([up2[PLANE:], down2[:HALF]])
    up3, down3, got3 = together(to_z(up2, 1), to_z(down2, -1), swap(late2, "level", 2))
    late_to_core(near, got2, 0, 1, 7)
    early_pair_to_core(up2[:PLANE], down2[HALF:], 1, 7)
    late3 = jnp.concatenate([up3[PLANE:], down3[:HALF]])
    up4, down4, got4 = together(
        to_z(up3[: PLANE + QUARTER], 1), to_z(down3[QUARTER:], -1), swap(late3, "level", 2)
    )
    late_to_core(late2, got3, 2, 6)
    early_pair_to_core(up3[:PLANE], down3[HALF:], 2, 6)
    late4 = jnp.concatenate([up4[PLANE:], down4[:QUARTER]])
    up5, down5 = together(
        to_z(jnp.concatenate([up4[:HALF], got4[:QUARTER]]), 1),
        to_z(jnp.concatenate([got4[HALF + QUARTER :], down4[QUARTER + HALF :]]), -1),
    )
    late_to_core(late3, got4, 3, 5)
    early_pair_to_core(up4[:PLANE], down4[QUARTER:], 3, 5)
    early_to_core(jnp.concatenate([up5[:HALF], down5[QUARTER:]]), (FAR, 0, 0, PLANE))
    late_to_core(late4, jnp.concatenate([up5[HALF:], down5[:QUARTER]]), FAR)
    return full, far, up1


def near_kernel(x, w_own, w_other, w_value, total):
    heads = w_own.shape[1]

    @pl.when(pl.program_id(0) == 0)
    def _():
        total[...] = jnp.zeros_like(total)

    part = x[...]
    for i, w in enumerate((w_own, w_other, w_value)):
        total[:, i * heads : (i + 1) * heads] += dot(part, w[...])


def far_kernel(info, x, w_own, w_other, w_value, total, query, key_value):
    sec, heads = query.shape
    part = x[...]
    own, other, value = (
        total[:, i * heads : (i + 1) * heads] + dot(part, w[...])
        for i, w in enumerate((w_own, w_other, w_value))
    )
    query[...] = jnp.where(info[0] == 0, own, other).astype(BF16)
    key_value[0, :sec] = jnp.where(info[0] == 0, other, own).astype(BF16)
    key_value[1, :sec] = value.astype(BF16)
    shape = (SHARE, heads)
    high, offset = info[1] // RADIX, info[2]
    left = lax.broadcasted_iota(jnp.int32, shape, 1) < HD
    key_value[0, sec:] = jnp.where(left, high, offset).astype(FLOAT).astype(BF16)
    key_value[1, sec:] = jnp.full(shape, info[1] - high * RADIX).astype(FLOAT).astype(BF16)


def project(info, rows, full, far):
    sec, heads = rows.shape[0], far[0].shape[1]
    weights = pl.BlockSpec((PLANE, heads), lambda i: (i, 0))
    sums = jax.ShapeDtypeStruct((sec, 3 * heads), FLOAT)
    total = pl.pallas_call(
        near_kernel,
        grid=(PLANES - 1,),
        out_shape=sums,
        in_specs=[
            pl.BlockSpec((sec, PLANE), lambda i: (0, jnp.where(i < FAR, i, i + 1))),
            weights,
            weights,
            weights,
        ],
        out_specs=pl.BlockSpec(sums.shape, lambda i: (0, 0)),
        compiler_params=pltpu.CompilerParams(vmem_limit_bytes=16 * 2**20),
        cost_estimate=pl.CostEstimate(
            flops=6 * sec * (D - PLANE) * heads,
            bytes_accessed=6 * (D - PLANE) * heads + 2 * sec * D,
            transcendentals=0,
        ),
    )(rows, *full[:3])
    whole = pl.BlockSpec((PLANE, heads), lambda i: (0, 0))
    return pl.pallas_call(
        far_kernel,
        grid=(1,),
        out_shape=(
            jax.ShapeDtypeStruct((sec, heads), BF16),
            jax.ShapeDtypeStruct((2, sec + SHARE, heads), BF16),
        ),
        in_specs=[
            pl.BlockSpec(memory_space=pltpu.SMEM),
            pl.BlockSpec((sec, PLANE), lambda i: (0, FAR)),
            whole,
            whole,
            whole,
            pl.BlockSpec(sums.shape, lambda i: (0, 0)),
        ],
        out_specs=(
            pl.BlockSpec((sec, heads), lambda i: (0, 0)),
            pl.BlockSpec((2, sec + SHARE, heads), lambda i: (0, 0, 0)),
        ),
        compiler_params=pltpu.CompilerParams(vmem_limit_bytes=16 * 2**20),
        cost_estimate=pl.CostEstimate(
            flops=6 * sec * PLANE * heads, bytes_accessed=6 * PLANE * heads, transcendentals=0
        ),
    )(info, rows, *far[:3], total)


def attend_kernel(info, query, low, mid, high, w_near, w_far, *refs):
    outs, attended = refs[:8], refs[8]
    offset, tensor_id, first, last = (info[i] for i in range(2, 6))
    sec = query.shape[0]

    @pl.when(pl.program_id(0) == 0)
    def _():
        place = lax.broadcasted_iota(jnp.int32, (1, 3 * sec), 1)
        rows = place ^ (tensor_id * SHARE)
        live = (rows >= offset) & (rows < offset + 2 * sec)
        live = live & ((rows >= sec) | (first == 0)) & ((rows < 2 * sec) | (last == 0))
        for head in range(query.shape[1] // HD):
            cols = slice(head * HD, (head + 1) * HD)
            keys = jnp.concatenate([a[0, :sec, cols] for a in (low, mid, high)], axis=0)
            values = jnp.concatenate([a[1, :sec, cols] for a in (low, mid, high)], axis=0)
            scores = dot_t(query[:, cols], keys) * (1.0 / math.sqrt(HD))
            scores = jnp.where(live, scores, -1e30)
            top = jnp.max(scores, axis=-1, keepdims=True)
            expo = jnp.where(live, jnp.exp(scores - top), 0.0)
            probs = (expo * (1.0 / jnp.sum(expo, axis=-1, keepdims=True))).astype(BF16)
            attended[:, cols] = dot(probs, values).astype(BF16)

    def write(w_out):
        part = dot_t(attended[...], w_out[...]).astype(BF16)
        for d in range(8):
            outs[d][...] = part[d * SHARE : (d + 1) * SHARE]

    @pl.when(pl.program_id(0) < PLANES - 1)
    def _():
        write(w_near)

    @pl.when(pl.program_id(0) == PLANES - 1)
    def _():
        write(w_far)


def attend(info, query, low, mid, high, w_near, w_far):
    sec, heads = query.shape
    rows = pl.BlockSpec(low.shape, lambda s: (0, 0, 0))
    return pl.pallas_call(
        attend_kernel,
        grid=(PLANES,),
        out_shape=tuple(jax.ShapeDtypeStruct((SHARE, D), BF16) for _ in range(8)),
        in_specs=[
            pl.BlockSpec(memory_space=pltpu.SMEM),
            pl.BlockSpec((sec, heads), lambda s: (0, 0)),
            rows,
            rows,
            rows,
            pl.BlockSpec((PLANE, heads), lambda s: (jnp.minimum(s, PLANES - 2), 0)),
            pl.BlockSpec((PLANE, heads), lambda s: (0, 0)),
        ],
        out_specs=tuple(
            pl.BlockSpec(
                (SHARE, PLANE),
                lambda s: (0, jnp.where(s < FAR, s, jnp.where(s == PLANES - 1, FAR, s + 1))),
            )
            for _ in range(8)
        ),
        scratch_shapes=[pltpu.VMEM((sec, heads), BF16)],
        compiler_params=pltpu.CompilerParams(vmem_limit_bytes=16 * 2**20),
        cost_estimate=pl.CostEstimate(
            flops=2 * sec * D * heads + 12 * sec * sec * heads,
            bytes_accessed=2 * D * heads + 2 * sec * D,
            transcendentals=3 * sec * heads,
        ),
    )(info, query, low, mid, high, w_near, w_far)


def normalize(x_float, emb, mod_table):
    mean = jnp.mean(x_float, axis=-1, keepdims=True)
    var = jnp.mean((x_float - mean) ** 2, axis=-1, keepdims=True)
    unit = (x_float - mean) / jnp.sqrt(var + 1e-06)
    return (unit * (1.0 + mod_table[1] + 0.5 * emb) + mod_table[0] + emb).astype(BF16)


def exchange(blocks):
    got = together(*[swap(blocks[d], "tensor", d) for d in SENDS])
    return [got[SENDS.index(d)] for d in range(1, 8)]


def shards(queue, tail_noise, timesteps, offsets, mod_table, w_query, w_key, w_value, w_out):
    level_id = lax.axis_index("level")
    level_count = lax.axis_size("level")
    tensor_id = lax.axis_index("tensor")
    groups = lax.axis_size("tensor")
    z, y_hi, core = level_id // 4, (level_id // 2) % 2, level_id % 2

    full, far, first_come = gather_weights(
        w_query, w_key, w_value, w_out.T, y_hi, core
    )
    queue, timesteps, offsets, _ = together(queue, timesteps, offsets, first_come)
    t_now, offset = timesteps[0], offsets[0]
    emb = embed(t_now)

    def rolled(a):
        parts = [
            lax.dynamic_slice_in_dim(a, ((z - s) % PLANES) * PLANE, PLANE, 1)
            for s in range(PLANES)
        ]
        return jnp.concatenate(parts, axis=1)

    normed = rolled(normalize(queue.astype(FLOAT), emb, mod_table))
    rows = jnp.concatenate(
        [
            lax.dynamic_slice_in_dim(normed, (tensor_id ^ d) * SHARE, SHARE, 0)
            for d in range(groups)
        ]
    )
    current = lax.dynamic_slice_in_dim(queue, tensor_id * SHARE, SHARE, 0)
    vel_list = []
    for step in range(2):
        section = (level_id - step) % level_count
        ends = [(section == end).astype(jnp.int32) for end in (0, level_count - 1)]
        info = jnp.stack([core, t_now, offset, tensor_id, *ends])
        gate = mod_table[2] + emb
        delta = sigma_of(jnp.maximum(t_now - TSTEPS // level_count, 0)) - sigma_of(t_now)

        query, mid = project(info, rows, full, far)
        low, high = together(moved(mid, 1), moved(mid, -1))
        parts = attend(info, query, low, mid, high, full[3], far[3])
        proj = parts[0].astype(FLOAT)
        for part in exchange(parts):
            proj = proj + part.astype(FLOAT)
        vel = gate * rolled(proj)
        updated = (current.astype(FLOAT) + delta * vel).astype(BF16)
        vel_list.append(vel.astype(BF16))
        if step == 0:
            t_now = (low[0, -1, 0].astype(FLOAT) * RADIX + low[1, -1, 0].astype(FLOAT)).astype(jnp.int32)
            offset = low[0, -1, -1].astype(jnp.int32)
            emb = embed(t_now)
            current = jnp.where(level_id == 0, tail_noise[0], updated)
            mine = rolled(normalize(current.astype(FLOAT), emb, mod_table))
            rows = jnp.concatenate([mine, *exchange([mine] * groups)])
    final, vel_list[1] = together(moved(updated, -2), moved(vel_list[1], -1))
    final = jnp.where(level_id == level_count - 1, tail_noise[1], final)
    return (final, jnp.stack(vel_list))


def solution(mesh):
    in_specs = (
        P("level", None),
        P(None, "tensor", None),
        P("level"),
        P("level"),
        P(),
        P("level", "tensor"),
        P("level", "tensor"),
        P("level", "tensor"),
        P("tensor", "level"),
    )
    out_specs = (P(("level", "tensor"), None), P(None, ("level", "tensor"), None))
    return jax.shard_map(shards, mesh=mesh, in_specs=in_specs, out_specs=out_specs, check_vma=False)
```

```python
import math

import jax
import jax.numpy as jnp
from jax import lax
from jax.experimental import pallas as pl
from jax.experimental.pallas import tpu as pltpu
from jax.sharding import PartitionSpec as P

D = 5120
HD = 128
TSTEPS = 1000
PLANES = 8
PLANE = D // PLANES
HALF = PLANE // 2
QUARTER = PLANE // 4
SHARE = 16
FAR = 4
SENDS = (1, 5, 4, 7, 3, 6, 2)
RADIX = 32
FLOAT = jnp.float32
BF16 = jnp.bfloat16


def sigma_of(t_index):
    unit = t_index.astype(FLOAT) / TSTEPS
    return 5.0 * unit / (1.0 + 4.0 * unit)


def embed(t_index):
    half = D // 2
    freqs = jnp.exp(-math.log(10000.0) * jnp.arange(half, dtype=FLOAT) / half)
    angles = t_index.astype(FLOAT) * freqs
    return jnp.concatenate([jnp.sin(angles), jnp.cos(angles)])


def dot(a, b):
    return jnp.dot(a, b, preferred_element_type=FLOAT)


def dot_t(a, b):
    return lax.dot_general(a, b, (((1,), (1,)), ((), ())), preferred_element_type=FLOAT)


def to_z(block, hops):
    count = lax.axis_size("level")
    return lax.ppermute(block, "level", [(i, (i + 4 * hops) % count) for i in range(count)])


def swap(block, axis, bit):
    return lax.ppermute(block, axis, [(i, i ^ bit) for i in range(lax.axis_size(axis))])


def moved(block, distance):
    count = lax.axis_size("level")
    return lax.ppermute(block, "level", [(i, (i + distance) % count) for i in range(count)])


def in_order(own, other, bit, axis=0):
    return jnp.where(
        bit == 0,
        jnp.concatenate([own, other], axis=axis),
        jnp.concatenate([other, own], axis=axis),
    )


def together(*arrays):
    return lax.optimization_barrier(arrays)


def gather_weights(w_query, w_key, w_value, w_out_t, y_hi, core):
    mine = jnp.where(core == 0, w_query, w_key)
    early = in_order(mine, swap(jnp.where(core == 0, w_key, w_query), "level", 1), core)
    mine = jnp.where(core == 0, w_value, w_out_t)
    late = in_order(mine, swap(jnp.where(core == 0, w_out_t, w_value), "level", 1), core)
    wide = late.shape[1]
    early, late = together(early, late)
    near_planes = D - PLANE
    full = [jnp.zeros((near_planes, wide), BF16) for _ in range(4)]
    far = [None] * 4

    def put(index, block, row):
        if row == FAR * PLANE:
            far[index] = block
        else:
            row = row - PLANE if row > FAR * PLANE else row
            full[index] = lax.dynamic_update_slice(full[index], block, (row, 0))

    def to_core(early_parts, early_planes, own, got, late_planes):
        shape = (len(late_planes), HALF, wide)
        late_block = in_order(own.reshape(shape), got.reshape(shape), y_hi, axis=1)
        late_block = late_block.reshape(len(late_planes) * PLANE, wide)
        block = jnp.concatenate([*early_parts, late_block])
        other = swap(block, "level", 1)
        for i, s in enumerate([*early_planes, *late_planes]):
            here, there = (a[i * PLANE : (i + 1) * PLANE] for a in (block, other))
            if i < len(early_planes):
                put(0, here, s * PLANE)
                put(1, there, s * PLANE)
            else:
                put(2, jnp.where(core == 0, here, there), s * PLANE)
                put(3, jnp.where(core == 0, there, here), s * PLANE)

    crossing, up1, down1 = together(swap(early, "level", 2), to_z(late, 1), to_z(late, -1))
    whole = in_order(early, crossing, y_hi)
    near = jnp.concatenate([late, up1, down1])
    up2, down2, got2 = together(
        to_z(jnp.concatenate([whole, up1]), 1),
        to_z(jnp.concatenate([down1, whole]), -1),
        swap(near, "level", 2),
    )
    late2 = jnp.concatenate([up2[PLANE:], down2[:HALF]])
    up3, down3, got3 = together(to_z(up2, 1), to_z(down2, -1), swap(late2, "level", 2))
    to_core((whole, up2[:PLANE], down2[HALF:]), (0, 1, 7), near, got2, (0, 1, 7))
    late3 = jnp.concatenate([up3[PLANE:], down3[:HALF]])
    up4, down4, got4 = together(
        to_z(up3[: PLANE + QUARTER], 1), to_z(down3[QUARTER:], -1), swap(late3, "level", 2)
    )
    to_core((up3[:PLANE], down3[HALF:]), (2, 6), late2, got3, (2, 6))
    late4 = jnp.concatenate([up4[PLANE:], down4[:QUARTER]])
    up5, down5 = together(
        to_z(jnp.concatenate([up4[:HALF], got4[:QUARTER]]), 1),
        to_z(jnp.concatenate([got4[HALF + QUARTER :], down4[QUARTER + HALF :]]), -1),
    )
    to_core((up4[:PLANE], down4[QUARTER:]), (3, 5), late3, got4, (3, 5))
    got5 = jnp.concatenate([up5[HALF:], down5[:QUARTER]])
    to_core((up5[:HALF], down5[QUARTER:]), (FAR,), late4, got5, (FAR,))
    return full, far, up1


def near_kernel(x, w_own, w_other, w_value, total):
    heads = w_own.shape[1]

    @pl.when(pl.program_id(0) == 0)
    def _():
        total[...] = jnp.zeros_like(total)

    part = x[...]
    for i, w in enumerate((w_own, w_other, w_value)):
        total[:, i * heads : (i + 1) * heads] += dot(part, w[...])


def far_kernel(info, x, w_own, w_other, w_value, total, query, key_value):
    sec, heads = query.shape
    part = x[...]
    own, other, value = (
        total[:, i * heads : (i + 1) * heads] + dot(part, w[...])
        for i, w in enumerate((w_own, w_other, w_value))
    )
    query[...] = jnp.where(info[0] == 0, own, other).astype(BF16)
    key_value[0, :sec] = jnp.where(info[0] == 0, other, own).astype(BF16)
    key_value[1, :sec] = value.astype(BF16)
    shape = (SHARE, heads)
    high, offset = info[1] // RADIX, info[2]
    left = lax.broadcasted_iota(jnp.int32, shape, 1) < HD
    key_value[0, sec:] = jnp.where(left, high, offset).astype(FLOAT).astype(BF16)
    key_value[1, sec:] = jnp.full(shape, info[1] - high * RADIX).astype(FLOAT).astype(BF16)


def project(info, rows, full, far):
    sec, heads = rows.shape[0], far[0].shape[1]
    weights = pl.BlockSpec((PLANE, heads), lambda i: (i, 0))
    sums = jax.ShapeDtypeStruct((sec, 3 * heads), FLOAT)
    total = pl.pallas_call(
        near_kernel,
        grid=(PLANES - 1,),
        out_shape=sums,
        in_specs=[
            pl.BlockSpec((sec, PLANE), lambda i: (0, jnp.where(i < FAR, i, i + 1))),
            weights,
            weights,
            weights,
        ],
        out_specs=pl.BlockSpec(sums.shape, lambda i: (0, 0)),
        compiler_params=pltpu.CompilerParams(vmem_limit_bytes=16 * 2**20),
        cost_estimate=pl.CostEstimate(
            flops=6 * sec * (D - PLANE) * heads,
            bytes_accessed=6 * (D - PLANE) * heads + 2 * sec * D,
            transcendentals=0,
        ),
    )(rows, *full[:3])
    whole = pl.BlockSpec((PLANE, heads), lambda i: (0, 0))
    return pl.pallas_call(
        far_kernel,
        grid=(1,),
        out_shape=(
            jax.ShapeDtypeStruct((sec, heads), BF16),
            jax.ShapeDtypeStruct((2, sec + SHARE, heads), BF16),
        ),
        in_specs=[
            pl.BlockSpec(memory_space=pltpu.SMEM),
            pl.BlockSpec((sec, PLANE), lambda i: (0, FAR)),
            whole,
            whole,
            whole,
            pl.BlockSpec(sums.shape, lambda i: (0, 0)),
        ],
        out_specs=(
            pl.BlockSpec((sec, heads), lambda i: (0, 0)),
            pl.BlockSpec((2, sec + SHARE, heads), lambda i: (0, 0, 0)),
        ),
        compiler_params=pltpu.CompilerParams(vmem_limit_bytes=16 * 2**20),
        cost_estimate=pl.CostEstimate(
            flops=6 * sec * PLANE * heads, bytes_accessed=6 * PLANE * heads, transcendentals=0
        ),
    )(info, rows, *far[:3], total)


def attend_kernel(info, query, low, mid, high, w_near, w_far, *refs):
    outs, attended = refs[:8], refs[8]
    offset, tensor_id, first, last = (info[i] for i in range(2, 6))
    sec = query.shape[0]

    @pl.when(pl.program_id(0) == 0)
    def _():
        place = lax.broadcasted_iota(jnp.int32, (1, 3 * sec), 1)
        rows = place ^ (tensor_id * SHARE)
        live = (rows >= offset) & (rows < offset + 2 * sec)
        live = live & ((rows >= sec) | (first == 0)) & ((rows < 2 * sec) | (last == 0))
        for head in range(query.shape[1] // HD):
            cols = slice(head * HD, (head + 1) * HD)
            keys = jnp.concatenate([a[0, :sec, cols] for a in (low, mid, high)], axis=0)
            values = jnp.concatenate([a[1, :sec, cols] for a in (low, mid, high)], axis=0)
            scores = dot_t(query[:, cols], keys) * (1.0 / math.sqrt(HD))
            scores = jnp.where(live, scores, -1e30)
            top = jnp.max(scores, axis=-1, keepdims=True)
            expo = jnp.where(live, jnp.exp(scores - top), 0.0)
            probs = (expo * (1.0 / jnp.sum(expo, axis=-1, keepdims=True))).astype(BF16)
            attended[:, cols] = dot(probs, values).astype(BF16)

    def write(w_out):
        part = dot_t(attended[...], w_out[...]).astype(BF16)
        for d in range(8):
            outs[d][...] = part[d * SHARE : (d + 1) * SHARE]

    @pl.when(pl.program_id(0) < PLANES - 1)
    def _():
        write(w_near)

    @pl.when(pl.program_id(0) == PLANES - 1)
    def _():
        write(w_far)


def attend(info, query, low, mid, high, w_near, w_far):
    sec, heads = query.shape
    rows = pl.BlockSpec(low.shape, lambda s: (0, 0, 0))
    return pl.pallas_call(
        attend_kernel,
        grid=(PLANES,),
        out_shape=tuple(jax.ShapeDtypeStruct((SHARE, D), BF16) for _ in range(8)),
        in_specs=[
            pl.BlockSpec(memory_space=pltpu.SMEM),
            pl.BlockSpec((sec, heads), lambda s: (0, 0)),
            rows,
            rows,
            rows,
            pl.BlockSpec((PLANE, heads), lambda s: (jnp.minimum(s, PLANES - 2), 0)),
            pl.BlockSpec((PLANE, heads), lambda s: (0, 0)),
        ],
        out_specs=tuple(
            pl.BlockSpec(
                (SHARE, PLANE),
                lambda s: (0, jnp.where(s < FAR, s, jnp.where(s == PLANES - 1, FAR, s + 1))),
            )
            for _ in range(8)
        ),
        scratch_shapes=[pltpu.VMEM((sec, heads), BF16)],
        compiler_params=pltpu.CompilerParams(vmem_limit_bytes=16 * 2**20),
        cost_estimate=pl.CostEstimate(
            flops=2 * sec * D * heads + 12 * sec * sec * heads,
            bytes_accessed=2 * D * heads + 2 * sec * D,
            transcendentals=3 * sec * heads,
        ),
    )(info, query, low, mid, high, w_near, w_far)


def normalize(x_float, emb, mod_table):
    mean = jnp.mean(x_float, axis=-1, keepdims=True)
    var = jnp.mean((x_float - mean) ** 2, axis=-1, keepdims=True)
    unit = (x_float - mean) / jnp.sqrt(var + 1e-06)
    return (unit * (1.0 + mod_table[1] + 0.5 * emb) + mod_table[0] + emb).astype(BF16)


def exchange(blocks):
    got = together(*[swap(blocks[d], "tensor", d) for d in SENDS])
    return [got[SENDS.index(d)] for d in range(1, 8)]


def shards(queue, tail_noise, timesteps, offsets, mod_table, w_query, w_key, w_value, w_out):
    level_id = lax.axis_index("level")
    level_count = lax.axis_size("level")
    tensor_id = lax.axis_index("tensor")
    groups = lax.axis_size("tensor")
    z, y_hi, core = level_id // 4, (level_id // 2) % 2, level_id % 2

    full, far, first_come = gather_weights(
        w_query, w_key, w_value, w_out.T, y_hi, core
    )
    queue, timesteps, offsets, _ = together(queue, timesteps, offsets, first_come)
    t_now, offset = timesteps[0], offsets[0]
    emb = embed(t_now)

    def rolled(a):
        parts = [
            lax.dynamic_slice_in_dim(a, ((z - s) % PLANES) * PLANE, PLANE, 1)
            for s in range(PLANES)
        ]
        return jnp.concatenate(parts, axis=1)

    normed = rolled(normalize(queue.astype(FLOAT), emb, mod_table))
    rows = jnp.concatenate(
        [
            lax.dynamic_slice_in_dim(normed, (tensor_id ^ d) * SHARE, SHARE, 0)
            for d in range(groups)
        ]
    )
    current = lax.dynamic_slice_in_dim(queue, tensor_id * SHARE, SHARE, 0)
    vel_list = []
    for step in range(2):
        section = (level_id - step) % level_count
        ends = [(section == end).astype(jnp.int32) for end in (0, level_count - 1)]
        info = jnp.stack([core, t_now, offset, tensor_id, *ends])
        gate = mod_table[2] + emb
        delta = sigma_of(jnp.maximum(t_now - TSTEPS // level_count, 0)) - sigma_of(t_now)

        query, mid = project(info, rows, full, far)
        low, high = together(moved(mid, 1), moved(mid, -1))
        parts = attend(info, query, low, mid, high, full[3], far[3])
        proj = parts[0].astype(FLOAT)
        for part in exchange(parts):
            proj = proj + part.astype(FLOAT)
        vel = gate * rolled(proj)
        updated = (current.astype(FLOAT) + delta * vel).astype(BF16)
        vel_list.append(vel.astype(BF16))
        if step == 0:
            t_now = (low[0, -1, 0].astype(FLOAT) * RADIX + low[1, -1, 0].astype(FLOAT)).astype(jnp.int32)
            offset = low[0, -1, -1].astype(jnp.int32)
            emb = embed(t_now)
            current = jnp.where(level_id == 0, tail_noise[0], updated)
            mine = rolled(normalize(current.astype(FLOAT), emb, mod_table))
            rows = jnp.concatenate([mine, *exchange([mine] * groups)])
    final, vel_list[1] = together(moved(updated, -2), moved(vel_list[1], -1))
    final = jnp.where(level_id == level_count - 1, tail_noise[1], final)
    return (final, jnp.stack(vel_list))


def solution(mesh):
    in_specs = (
        P("level", None),
        P(None, "tensor", None),
        P("level"),
        P("level"),
        P(),
        P("level", "tensor"),
        P("level", "tensor"),
        P("level", "tensor"),
        P("tensor", "level"),
    )
    out_specs = (P(("level", "tensor"), None), P(None, ("level", "tensor"), None))
    return jax.shard_map(shards, mesh=mesh, in_specs=in_specs, out_specs=out_specs, check_vma=False)
```

```python
import math

import jax
import jax.numpy as jnp
from jax import lax
from jax.experimental import pallas as pl
from jax.experimental.pallas import tpu as pltpu
from jax.sharding import PartitionSpec as P

D = 5120
HD = 128
TSTEPS = 1000
PLANES = 8
PLANE = D // PLANES
HALF = PLANE // 2
QUARTER = PLANE // 4
SHARE = 16
FAR = 4
SENDS = (4, 5, 6, 7, 3, 2, 1)
RADIX = 32
FLOAT = jnp.float32
BF16 = jnp.bfloat16


def sigma_of(t_index):
    unit = t_index.astype(FLOAT) / TSTEPS
    return 5.0 * unit / (1.0 + 4.0 * unit)


def embed(t_index):
    half = D // 2
    freqs = jnp.exp(-math.log(10000.0) * jnp.arange(half, dtype=FLOAT) / half)
    angles = t_index.astype(FLOAT) * freqs
    return jnp.concatenate([jnp.sin(angles), jnp.cos(angles)])


def dot(a, b):
    return jnp.dot(a, b, preferred_element_type=FLOAT)


def dot_t(a, b):
    return lax.dot_general(a, b, (((1,), (1,)), ((), ())), preferred_element_type=FLOAT)


def to_z(block, hops):
    count = lax.axis_size("level")
    return lax.ppermute(block, "level", [(i, (i + 4 * hops) % count) for i in range(count)])


def swap(block, axis, bit):
    return lax.ppermute(block, axis, [(i, i ^ bit) for i in range(lax.axis_size(axis))])


def moved(block, distance):
    count = lax.axis_size("level")
    return lax.ppermute(block, "level", [(i, (i + distance) % count) for i in range(count)])


def in_order(own, other, bit, axis=0):
    return jnp.where(
        bit == 0,
        jnp.concatenate([own, other], axis=axis),
        jnp.concatenate([other, own], axis=axis),
    )


def together(*arrays):
    return lax.optimization_barrier(arrays)


def gather_weights(w_query, w_key, w_value, w_out_t, y_hi, core):
    mine = jnp.where(core == 0, w_query, w_key)
    early = in_order(mine, swap(jnp.where(core == 0, w_key, w_query), "level", 1), core)
    mine = jnp.where(core == 0, w_value, w_out_t)
    late = in_order(mine, swap(jnp.where(core == 0, w_out_t, w_value), "level", 1), core)
    wide = late.shape[1]
    early, late = together(early, late)
    near_planes = D - PLANE
    full = [jnp.zeros((near_planes, wide), BF16) for _ in range(4)]
    far = [None] * 4

    def put(index, block, row):
        if row == FAR * PLANE:
            far[index] = block
        else:
            row = row - PLANE if row > FAR * PLANE else row
            full[index] = lax.dynamic_update_slice(full[index], block, (row, 0))

    def to_core(early_parts, early_planes, own, got, late_planes):
        shape = (len(late_planes), HALF, wide)
        late_block = in_order(own.reshape(shape), got.reshape(shape), y_hi, axis=1)
        late_block = late_block.reshape(len(late_planes) * PLANE, wide)
        block = jnp.concatenate([*early_parts, late_block])
        other = swap(block, "level", 1)
        for i, s in enumerate([*early_planes, *late_planes]):
            here, there = (a[i * PLANE : (i + 1) * PLANE] for a in (block, other))
            if i < len(early_planes):
                put(0, here, s * PLANE)
                put(1, there, s * PLANE)
            else:
                put(2, jnp.where(core == 0, here, there), s * PLANE)
                put(3, jnp.where(core == 0, there, here), s * PLANE)

    crossing, up1, down1 = together(swap(early, "level", 2), to_z(late, 1), to_z(late, -1))
    whole = in_order(early, crossing, y_hi)
    near = jnp.concatenate([late, up1, down1])
    up2, down2, got2 = together(
        to_z(jnp.concatenate([whole, up1]), 1),
        to_z(jnp.concatenate([down1, whole]), -1),
        swap(near, "level", 2),
    )
    late2 = jnp.concatenate([up2[PLANE:], down2[:HALF]])
    up3, down3, got3 = together(to_z(up2, 1), to_z(down2, -1), swap(late2, "level", 2))
    to_core((whole, up2[:PLANE], down2[HALF:]), (0, 1, 7), near, got2, (0, 1, 7))
    late3 = jnp.concatenate([up3[PLANE:], down3[:HALF]])
    up4, down4, got4 = together(
        to_z(up3[: PLANE + QUARTER], 1), to_z(down3[QUARTER:], -1), swap(late3, "level", 2)
    )
    to_core((up3[:PLANE], down3[HALF:]), (2, 6), late2, got3, (2, 6))
    late4 = jnp.concatenate([up4[PLANE:], down4[:QUARTER]])
    up5, down5 = together(
        to_z(jnp.concatenate([up4[:HALF], got4[:QUARTER]]), 1),
        to_z(jnp.concatenate([got4[HALF + QUARTER :], down4[QUARTER + HALF :]]), -1),
    )
    to_core((up4[:PLANE], down4[QUARTER:]), (3, 5), late3, got4, (3, 5))
    got5 = jnp.concatenate([up5[HALF:], down5[:QUARTER]])
    to_core((up5[:HALF], down5[QUARTER:]), (FAR,), late4, got5, (FAR,))
    return full, far, up1


def near_kernel(x, w_own, w_other, w_value, total):
    heads = w_own.shape[1]

    @pl.when(pl.program_id(0) == 0)
    def _():
        total[...] = jnp.zeros_like(total)

    part = x[...]
    for i, w in enumerate((w_own, w_other, w_value)):
        total[:, i * heads : (i + 1) * heads] += dot(part, w[...])


def far_kernel(info, x, w_own, w_other, w_value, total, query, key_value):
    sec, heads = query.shape
    part = x[...]
    own, other, value = (
        total[:, i * heads : (i + 1) * heads] + dot(part, w[...])
        for i, w in enumerate((w_own, w_other, w_value))
    )
    query[...] = jnp.where(info[0] == 0, own, other).astype(BF16)
    key_value[0, :sec] = jnp.where(info[0] == 0, other, own).astype(BF16)
    key_value[1, :sec] = value.astype(BF16)
    shape = (SHARE, heads)
    high, offset = info[1] // RADIX, info[2]
    left = lax.broadcasted_iota(jnp.int32, shape, 1) < HD
    key_value[0, sec:] = jnp.where(left, high, offset).astype(FLOAT).astype(BF16)
    key_value[1, sec:] = jnp.full(shape, info[1] - high * RADIX).astype(FLOAT).astype(BF16)


def project(info, rows, full, far):
    sec, heads = rows.shape[0], far[0].shape[1]
    weights = pl.BlockSpec((PLANE, heads), lambda i: (i, 0))
    sums = jax.ShapeDtypeStruct((sec, 3 * heads), FLOAT)
    total = pl.pallas_call(
        near_kernel,
        grid=(PLANES - 1,),
        out_shape=sums,
        in_specs=[
            pl.BlockSpec((sec, PLANE), lambda i: (0, jnp.where(i < FAR, i, i + 1))),
            weights,
            weights,
            weights,
        ],
        out_specs=pl.BlockSpec(sums.shape, lambda i: (0, 0)),
        compiler_params=pltpu.CompilerParams(vmem_limit_bytes=16 * 2**20),
        cost_estimate=pl.CostEstimate(
            flops=6 * sec * (D - PLANE) * heads,
            bytes_accessed=6 * (D - PLANE) * heads + 2 * sec * D,
            transcendentals=0,
        ),
    )(rows, *full[:3])
    whole = pl.BlockSpec((PLANE, heads), lambda i: (0, 0))
    return pl.pallas_call(
        far_kernel,
        grid=(1,),
        out_shape=(
            jax.ShapeDtypeStruct((sec, heads), BF16),
            jax.ShapeDtypeStruct((2, sec + SHARE, heads), BF16),
        ),
        in_specs=[
            pl.BlockSpec(memory_space=pltpu.SMEM),
            pl.BlockSpec((sec, PLANE), lambda i: (0, FAR)),
            whole,
            whole,
            whole,
            pl.BlockSpec(sums.shape, lambda i: (0, 0)),
        ],
        out_specs=(
            pl.BlockSpec((sec, heads), lambda i: (0, 0)),
            pl.BlockSpec((2, sec + SHARE, heads), lambda i: (0, 0, 0)),
        ),
        compiler_params=pltpu.CompilerParams(vmem_limit_bytes=16 * 2**20),
        cost_estimate=pl.CostEstimate(
            flops=6 * sec * PLANE * heads, bytes_accessed=6 * PLANE * heads, transcendentals=0
        ),
    )(info, rows, *far[:3], total)


def attend_kernel(info, query, low, mid, high, w_near, w_far, *refs):
    outs, attended = refs[:8], refs[8]
    offset, tensor_id, first, last = (info[i] for i in range(2, 6))
    sec = query.shape[0]

    @pl.when(pl.program_id(0) == 0)
    def _():
        place = lax.broadcasted_iota(jnp.int32, (1, 3 * sec), 1)
        rows = place ^ (tensor_id * SHARE)
        live = (rows >= offset) & (rows < offset + 2 * sec)
        live = live & ((rows >= sec) | (first == 0)) & ((rows < 2 * sec) | (last == 0))
        for head in range(query.shape[1] // HD):
            cols = slice(head * HD, (head + 1) * HD)
            keys = jnp.concatenate([a[0, :sec, cols] for a in (low, mid, high)], axis=0)
            values = jnp.concatenate([a[1, :sec, cols] for a in (low, mid, high)], axis=0)
            scores = dot_t(query[:, cols], keys) * (1.0 / math.sqrt(HD))
            scores = jnp.where(live, scores, -1e30)
            top = jnp.max(scores, axis=-1, keepdims=True)
            expo = jnp.where(live, jnp.exp(scores - top), 0.0)
            probs = (expo * (1.0 / jnp.sum(expo, axis=-1, keepdims=True))).astype(BF16)
            attended[:, cols] = dot(probs, values).astype(BF16)

    def write(w_out):
        part = dot_t(attended[...], w_out[...]).astype(BF16)
        for d in range(8):
            outs[d][...] = part[d * SHARE : (d + 1) * SHARE]

    @pl.when(pl.program_id(0) < PLANES - 1)
    def _():
        write(w_near)

    @pl.when(pl.program_id(0) == PLANES - 1)
    def _():
        write(w_far)


def attend(info, query, low, mid, high, w_near, w_far):
    sec, heads = query.shape
    rows = pl.BlockSpec(low.shape, lambda s: (0, 0, 0))
    return pl.pallas_call(
        attend_kernel,
        grid=(PLANES,),
        out_shape=tuple(jax.ShapeDtypeStruct((SHARE, D), BF16) for _ in range(8)),
        in_specs=[
            pl.BlockSpec(memory_space=pltpu.SMEM),
            pl.BlockSpec((sec, heads), lambda s: (0, 0)),
            rows,
            rows,
            rows,
            pl.BlockSpec((PLANE, heads), lambda s: (jnp.minimum(s, PLANES - 2), 0)),
            pl.BlockSpec((PLANE, heads), lambda s: (0, 0)),
        ],
        out_specs=tuple(
            pl.BlockSpec(
                (SHARE, PLANE),
                lambda s: (0, jnp.where(s < FAR, s, jnp.where(s == PLANES - 1, FAR, s + 1))),
            )
            for _ in range(8)
        ),
        scratch_shapes=[pltpu.VMEM((sec, heads), BF16)],
        compiler_params=pltpu.CompilerParams(vmem_limit_bytes=16 * 2**20),
        cost_estimate=pl.CostEstimate(
            flops=2 * sec * D * heads + 12 * sec * sec * heads,
            bytes_accessed=2 * D * heads + 2 * sec * D,
            transcendentals=3 * sec * heads,
        ),
    )(info, query, low, mid, high, w_near, w_far)


def normalize(x_float, emb, mod_table):
    mean = jnp.mean(x_float, axis=-1, keepdims=True)
    var = jnp.mean((x_float - mean) ** 2, axis=-1, keepdims=True)
    unit = (x_float - mean) / jnp.sqrt(var + 1e-06)
    return (unit * (1.0 + mod_table[1] + 0.5 * emb) + mod_table[0] + emb).astype(BF16)


def exchange(blocks):
    got = together(*[swap(blocks[d], "tensor", d) for d in SENDS])
    return [got[SENDS.index(d)] for d in range(1, 8)]


def shards(queue, tail_noise, timesteps, offsets, mod_table, w_query, w_key, w_value, w_out):
    level_id = lax.axis_index("level")
    level_count = lax.axis_size("level")
    tensor_id = lax.axis_index("tensor")
    groups = lax.axis_size("tensor")
    z, y_hi, core = level_id // 4, (level_id // 2) % 2, level_id % 2

    full, far, first_come = gather_weights(
        w_query, w_key, w_value, w_out.T, y_hi, core
    )
    queue, timesteps, offsets, _ = together(queue, timesteps, offsets, first_come)
    t_now, offset = timesteps[0], offsets[0]
    emb = embed(t_now)

    def rolled(a):
        parts = [
            lax.dynamic_slice_in_dim(a, ((z - s) % PLANES) * PLANE, PLANE, 1)
            for s in range(PLANES)
        ]
        return jnp.concatenate(parts, axis=1)

    normed = rolled(normalize(queue.astype(FLOAT), emb, mod_table))
    rows = jnp.concatenate(
        [
            lax.dynamic_slice_in_dim(normed, (tensor_id ^ d) * SHARE, SHARE, 0)
            for d in range(groups)
        ]
    )
    current = lax.dynamic_slice_in_dim(queue, tensor_id * SHARE, SHARE, 0)
    vel_list = []
    for step in range(2):
        section = (level_id - step) % level_count
        ends = [(section == end).astype(jnp.int32) for end in (0, level_count - 1)]
        info = jnp.stack([core, t_now, offset, tensor_id, *ends])
        gate = mod_table[2] + emb
        delta = sigma_of(jnp.maximum(t_now - TSTEPS // level_count, 0)) - sigma_of(t_now)

        query, mid = project(info, rows, full, far)
        low, high = together(moved(mid, 1), moved(mid, -1))
        parts = attend(info, query, low, mid, high, full[3], far[3])
        proj = parts[0].astype(FLOAT)
        for part in exchange(parts):
            proj = proj + part.astype(FLOAT)
        vel = gate * rolled(proj)
        updated = (current.astype(FLOAT) + delta * vel).astype(BF16)
        vel_list.append(vel.astype(BF16))
        if step == 0:
            t_now = (low[0, -1, 0].astype(FLOAT) * RADIX + low[1, -1, 0].astype(FLOAT)).astype(jnp.int32)
            offset = low[0, -1, -1].astype(jnp.int32)
            emb = embed(t_now)
            current = jnp.where(level_id == 0, tail_noise[0], updated)
            mine = rolled(normalize(current.astype(FLOAT), emb, mod_table))
            rows = jnp.concatenate([mine, *exchange([mine] * groups)])
    final, vel_list[1] = together(moved(updated, -2), moved(vel_list[1], -1))
    final = jnp.where(level_id == level_count - 1, tail_noise[1], final)
    return (final, jnp.stack(vel_list))


def solution(mesh):
    in_specs = (
        P("level", None),
        P(None, "tensor", None),
        P("level"),
        P("level"),
        P(),
        P("level", "tensor"),
        P("level", "tensor"),
        P("level", "tensor"),
        P("tensor", "level"),
    )
    out_specs = (P(("level", "tensor"), None), P(None, ("level", "tensor"), None))
    return jax.shard_map(shards, mesh=mesh, in_specs=in_specs, out_specs=out_specs, check_vma=False)
```
